32 devices in a mesh: dp: 4 (over x, core), nbr: 8 (over z, y).
Axes of the slice: x: 2, y: 2, z: 4, core: 2. Of those that a mesh axis runs over, the one named last changes fastest.
Arguments:
- tokens: bfloat16 [8, 1024, 768], P('nbr', 'dp'), may hold values from -6 to 6
- neighbours: bfloat16 [8, 4096, 768], P(None, ('dp', 'nbr')), may hold values from -6 to 6
- lengths: int32 [8], P('nbr'), may hold values from 512 to 1024, as said below
- slots: int32 [8, 16, 2], P('nbr', 'dp'), may hold values from 0 to 7, as said below
- grad_out: bfloat16 [8, 1024, 768], P('nbr', 'dp'), may hold values from -6 to 6
- w_query: float32 [768, 768], P(('dp', 'nbr')), may hold values from -0.21875 to 0.21875
- w_key: float32 [768, 768], P(('dp', 'nbr')), may hold values from -0.21875 to 0.21875
- w_value: float32 [768, 768], P(('dp', 'nbr')), may hold values from -0.21875 to 0.21875
- w_attn_out: float32 [768, 768], P(('dp', 'nbr')), may hold values from -1.75 to 1.75
- w_cross_query: float32 [768, 768], P(('dp', 'nbr')), may hold values from -0.21875 to 0.21875
- w_cross_key: float32 [768, 768], P(('dp', 'nbr')), may hold values from -0.21875 to 0.21875
- w_cross_value: float32 [768, 768], P(('dp', 'nbr')), may hold values from -0.21875 to 0.21875
- w_cross_out: float32 [768, 768], P(('dp', 'nbr')), may hold values from -2 to 2
- w_mlp_in: float32 [768, 3072], P(('dp', 'nbr')), may hold values from -0.21875 to 0.21875
- w_mlp_out: float32 [3072, 768], P(('dp', 'nbr')), may hold values from -0.109375 to 0.109375
- gain_attn: float32 [768], P(('dp', 'nbr')), may hold values from 0.25 to 1.75
- gain_cross: float32 [768], P(('dp', 'nbr')), may hold values from 0.25 to 1.75
- gain_mlp: float32 [768], P(('dp', 'nbr')), may hold values from 0.25 to 1.75
Outputs:
- output: bfloat16 [8, 1024, 768], P('nbr', 'dp')
- grad_tokens: bfloat16 [8, 1024, 768], P('nbr', 'dp')
- grad_neighbours: bfloat16 [8, 4096, 768], P(None, ('dp', 'nbr'))
- grad_w_query: float32 [768, 768], P(('dp', 'nbr'))
- grad_w_key: float32 [768, 768], P(('dp', 'nbr'))
- grad_w_value: float32 [768, 768], P(('dp', 'nbr'))
- grad_w_attn_out: float32 [768, 768], P(('dp', 'nbr'))
- grad_w_cross_query: float32 [768, 768], P(('dp', 'nbr'))
- grad_w_cross_key: float32 [768, 768], P(('dp', 'nbr'))
- grad_w_cross_value: float32 [768, 768], P(('dp', 'nbr'))
- grad_w_cross_out: float32 [768, 768], P(('dp', 'nbr'))
- grad_w_mlp_in: float32 [768, 3072], P(('dp', 'nbr'))
- grad_w_mlp_out: float32 [3072, 768], P(('dp', 'nbr'))
- grad_gain_attn: float32 [768], P(('dp', 'nbr'))
- grad_gain_cross: float32 [768], P(('dp', 'nbr'))
- grad_gain_mlp: float32 [768], P(('dp', 'nbr'))
The draws below stay inside these ranges and needn't reach their ends.
Inputs may be any that keep to these rules, and one draw needn't show every extreme that they name: `lengths`: the longest sequence of every draw has 1024 true tokens. For each sequence and each aligned block of 4 spans, the slots of those spans' neighbours are a permutation of 0 to 7.
All inputs are finite; a program needn't handle non-finite values.
Results may differ from the reference program's by a relative error of at most 0.03.
Values may be sent and summed in bfloat16 or wider, within the bound.
No kernel may reach another device: no remote copies, remote signals or barrier semaphores. Data moves between devices by JAX's collectives and lax.ppermute only.
A program may use at most 192 MiB of HBM per device.

```python
import jax
import jax.numpy as jnp
from jax import lax

D = 768
HEAD = 64
FF = 3072
SPAN = 64
NEIGH = 2
RET = 128
SEQS = 8
SEQLEN = 1024
CH_DEV = 4
NCH = 16
NTOK = 4096


def draw_lengths(key, part):
    first_key, second_key = jax.random.split(key)
    values = jax.random.randint(first_key, (SEQS,), SEQLEN // 2, SEQLEN + 1, dtype=jnp.int32)
    longest = jax.random.randint(second_key, (), 0, SEQS, dtype=jnp.int32)
    return jnp.where(jnp.arange(SEQS, dtype=jnp.int32) == longest, SEQLEN, values).astype(jnp.int32)


def draw_slots(key, part):
    entry_count = CH_DEV * NEIGH
    block_count = NCH // CH_DEV
    raw = jax.random.randint(key, (SEQS, block_count, entry_count), 0, 1048576, dtype=jnp.int32)
    distinct = raw * entry_count + jnp.arange(entry_count, dtype=jnp.int32)
    order = jnp.argsort(distinct, axis=-1, stable=True).astype(jnp.int32)
    return order.reshape(SEQS, NCH, NEIGH)


def levels(rng, shape, cuts, least, high):
    def one(dim, blocks):
        steps = jax.random.uniform(jax.random.fold_in(jax.random.fold_in(rng, 6), dim), (blocks,), jnp.float32, least / len(cuts), high / len(cuts))
        return jnp.repeat(jnp.exp(steps), shape[dim] // blocks).reshape((-1,) + (1,) * (len(shape) - dim - 1))

    loudness = one(*cuts[0])
    for cut in cuts[1:]:
        loudness = loudness * one(*cut)
    return loudness


def bell_draw(rng, dims, scale, reach, shards=(), held_as=jnp.bfloat16):
    values = scale * jax.random.normal(rng, dims, jnp.float32)
    if shards:
        values = values * levels(rng, dims, shards, -0.22, 0.18)
    return jnp.clip(values, -reach, reach).astype(held_as)


def setup_inputs(seed: int = 0) -> dict:
    keys = jax.random.split(jax.random.key(seed), 19)
    return {
        "tokens": bell_draw(keys[0], (SEQS, SEQLEN, D), 1.0, 6.0, ((0, 8), (1, 4))),
        "neighbours": bell_draw(keys[1], (SEQS, NTOK, D), 1.0, 6.0, ((1, 32),)),
        "lengths": draw_lengths(jax.random.fold_in(keys[18], 71), 0),
        "slots": draw_slots(jax.random.fold_in(keys[18], 71), 0),
        "grad_out": bell_draw(keys[4], (SEQS, SEQLEN, D), 1.0, 6.0, ((0, 8), (1, 4))),
        "w_query": bell_draw(keys[5], (D, D), D ** -0.5, 0.21875, ((0, 32),), jnp.float32),
        "w_key": bell_draw(keys[6], (D, D), D ** -0.5, 0.21875, ((0, 32),), jnp.float32),
        "w_value": bell_draw(keys[7], (D, D), D ** -0.5, 0.21875, ((0, 32),), jnp.float32),
        "w_attn_out": bell_draw(keys[8], (D, D), (D // 64) ** -0.5, 1.75, ((0, 32),), jnp.float32),
        "w_cross_query": bell_draw(keys[9], (D, D), D ** -0.5, 0.21875, ((0, 32),), jnp.float32),
        "w_cross_key": bell_draw(keys[10], (D, D), D ** -0.5, 0.21875, ((0, 32),), jnp.float32),
        "w_cross_value": bell_draw(keys[11], (D, D), D ** -0.5, 0.21875, ((0, 32),), jnp.float32),
        "w_cross_out": bell_draw(keys[12], (D, D), (D // 96) ** -0.5, 2.0, ((0, 32),), jnp.float32),
        "w_mlp_in": bell_draw(keys[13], (D, FF), D ** -0.5, 0.21875, ((0, 32),), jnp.float32),
        "w_mlp_out": bell_draw(keys[14], (FF, D), FF ** -0.5, 0.109375, ((0, 32),), jnp.float32),
        "gain_attn": jnp.clip(1.0 + 0.15 * jax.random.normal(keys[15], (D,), jnp.float32), 0.25, 1.75),
        "gain_cross": jnp.clip(1.0 + 0.15 * jax.random.normal(keys[16], (D,), jnp.float32), 0.25, 1.75),
        "gain_mlp": jnp.clip(1.0 + 0.15 * jax.random.normal(keys[17], (D,), jnp.float32), 0.25, 1.75),
    }


@jax.custom_vjp
def low(v):
    return lax.optimization_barrier(v.astype(jnp.bfloat16)).astype(jnp.float32)

@jax.custom_vjp
def low_back(v):
    return v

def low_keep(v):
    return (low(v), None)

def low_pass(kept, grad):
    return (grad,)

def back_keep(v):
    return (v, None)

def back_low(kept, grad):
    return (low(grad),)
low.defvjp(low_keep, low_pass)
low_back.defvjp(back_keep, back_low)
EPSILON = 1e-06
SCORE_SCALE = 0.125
MASKED = -1e+30
HIGHEST_PRECISION = lax.Precision.HIGHEST

def rms_gain(values, gain):
    return values * lax.rsqrt(lax.optimization_barrier(jnp.mean(values * values, axis=-1, keepdims=True)) + EPSILON) * gain

def product(left, right):
    return jnp.matmul(left, right, precision=HIGHEST_PRECISION)

def windows(table, slot_row, seq_length, head_count):
    blocks = seq_length // (CH_DEV * SPAN)
    entries = CH_DEV * NEIGH
    grouped = table.reshape(blocks, entries, RET * table.shape[-1])
    index = slot_row.reshape(blocks, entries)[:, :, None].astype(jnp.int32)
    picked = jnp.take_along_axis(grouped, index, axis=1)
    picked = picked.reshape(seq_length // SPAN, NEIGH * RET, head_count, HEAD)
    empty = jnp.zeros((1,) + picked.shape[1:], jnp.float32)
    return jnp.concatenate([empty, picked], axis=0)

def layer(inputs, encoded, params, length, slot_row):
    query_mat, key_mat, value_mat, attn_mat, cquery_mat, ckey_mat, cvalue_mat, cout_mat, upper_mat, lower_mat, gain_one, gain_two, gain_three = [low(weight) for weight in params]
    seq_length, model_width = inputs.shape
    head_count = model_width // HEAD
    h_one = low(rms_gain(inputs, gain_one))
    queries = low_back(low(product(h_one, query_mat))).reshape(seq_length, head_count, HEAD)
    key_rows = low_back(low(product(h_one, key_mat))).reshape(seq_length, head_count, HEAD)
    value_rows = low_back(low(product(h_one, value_mat))).reshape(seq_length, head_count, HEAD)
    scores = low_back(jnp.einsum('qhd,khd->hqk', queries, key_rows, precision=HIGHEST_PRECISION) * SCORE_SCALE)
    position = jnp.arange(seq_length)
    allowed = (position[None, :] <= position[:, None]) & (position[None, :] < length)
    probs = low(jax.nn.softmax(jnp.where(allowed[None], scores, MASKED), axis=-1))
    attended = jnp.einsum('hqk,khd->qhd', probs, value_rows, precision=HIGHEST_PRECISION)
    attended = low_back(low(attended.reshape(seq_length, model_width)))
    resid_one = inputs + low_back(product(attended, attn_mat))
    h_two = low(rms_gain(resid_one, gain_two))
    cross_queries = low_back(low(product(h_two, cquery_mat))).reshape(seq_length, head_count, HEAD)
    cross_keys = low_back(low(product(encoded, ckey_mat)))
    cross_values = low_back(low(product(encoded, cvalue_mat)))
    win_keys = windows(cross_keys, slot_row, seq_length, head_count)
    win_values = windows(cross_values, slot_row, seq_length, head_count)
    group_count = seq_length // SPAN + 1
    pad_queries = jnp.pad(cross_queries, ((1, SPAN - 1), (0, 0), (0, 0))).reshape(group_count, SPAN, head_count, HEAD)
    cross_scores = low_back(jnp.einsum('gqhd,gkhd->ghqk', pad_queries, win_keys, precision=HIGHEST_PRECISION) * SCORE_SCALE)
    cross_probs = low(jax.nn.softmax(cross_scores, axis=-1))
    cross_full = jnp.einsum('ghqk,gkhd->gqhd', cross_probs, win_values, precision=HIGHEST_PRECISION)
    cross_out = low_back(low(cross_full.reshape(group_count * SPAN, model_width)[1:1 + seq_length]))
    resid_two = resid_one + low_back(product(cross_out, cout_mat))
    h_three = low(rms_gain(resid_two, gain_three))
    upward = low_back(product(h_three, upper_mat))
    active = low(jax.nn.gelu(upward, approximate=True))
    return resid_two + low_back(product(active, lower_mat))

def reference(tokens, neighbours, lengths, slots, grad_out, w_query, w_key, w_value, w_attn_out, w_cross_query, w_cross_key, w_cross_value, w_cross_out, w_mlp_in, w_mlp_out, gain_attn, gain_cross, gain_mlp):
    params = (w_query, w_key, w_value, w_attn_out, w_cross_query, w_cross_key, w_cross_value, w_cross_out, w_mlp_in, w_mlp_out, gain_attn, gain_cross, gain_mlp)

    def seq_step(totals, seq_item):
        inputs, encoded, length, slot_row, cotangent = seq_item

        def forward(token_rows, nbr_rows, weights):
            return layer(token_rows, nbr_rows, weights, length, slot_row)
        result, pullback = jax.vjp(forward, inputs.astype(jnp.float32), encoded.astype(jnp.float32), params)
        grad_rows, grad_nbr, grad_params = pullback(cotangent.astype(jnp.float32))
        totals = jax.tree.map(jnp.add, totals, grad_params)
        return (totals, (result.astype(jnp.bfloat16), grad_rows.astype(jnp.bfloat16), grad_nbr.astype(jnp.bfloat16)))
    start = tuple((jnp.zeros_like(weight) for weight in params))
    totals, outputs = lax.scan(seq_step, start, (tokens, neighbours, lengths, slots, grad_out))
    return (outputs[0], outputs[1], outputs[2], totals[0], totals[1], totals[2], totals[3], totals[4], totals[5], totals[6], totals[7], totals[8], totals[9], totals[10], totals[11], totals[12])
```

```python
import functools

import jax
import jax.numpy as jnp
from jax import lax
from jax.experimental import pallas as pl
from jax.experimental.pallas import tpu as pltpu
from jax.sharding import PartitionSpec as P

HEAD = 64
SPAN = 64
NEIGH = 2
RET = 128
QUAD = 256
LANES = 128

EPSILON = 1e-06
SCALE = 0.125
MASKED = -1e30
GELU_C = 0.7978845608
GELU_D = 0.044715

BF = jnp.bfloat16
F32 = jnp.float32
VMEM_LIMIT = 60 * 1024 * 1024

U_Q, U_K, U_V, U_O, U_CQ, U_CK, U_CV, U_CO, U_IN = range(9)


def nn(a, b):
    return lax.dot_general(a, b, (((1,), (0,)), ((), ())), preferred_element_type=F32)


def nt(a, b):
    return lax.dot_general(a, b, (((1,), (1,)), ((), ())), preferred_element_type=F32)


def tn(a, b):
    return lax.dot_general(a, b, (((0,), (0,)), ((), ())), preferred_element_type=F32)


def inv_rms(x):
    return lax.rsqrt(jnp.mean(x * x, axis=-1, keepdims=True) + EPSILON)


def rms_back(x, gain, dz):
    r = inv_rms(x)
    n = x * r
    dzg = dz * gain
    dx = r * (dzg - n * jnp.mean(dzg * n, axis=-1, keepdims=True))
    return dx, dz * n


def column_sum(values, column):
    rows = values.shape[0]
    pick = (lax.broadcasted_iota(jnp.int32, (rows, LANES), 1) == column).astype(BF)
    high = values.astype(BF)
    low = (values - high.astype(F32)).astype(BF)
    return tn(high, pick) + tn(low, pick)


def head_lane(rows):
    return lax.broadcasted_iota(jnp.int32, (rows, QUAD), 1) // HEAD


def only_head(x, h):
    return jnp.where(head_lane(x.shape[0]) == h, x, jnp.zeros_like(x))


def by_heads(x):
    return jnp.concatenate([only_head(x, h) for h in range(QUAD // HEAD)], axis=0)


def from_heads(x):
    rows = x.shape[0] // (QUAD // HEAD)
    lane = head_lane(rows)
    out = x[:rows]
    for h in range(1, QUAD // HEAD):
        out = jnp.where(lane == h, x[h * rows : (h + 1) * rows], out)
    return out


def self_bias(place, length, rows, key_count):
    shape = (rows, key_count)
    key = lax.broadcasted_iota(jnp.int32, shape, 1)
    key_pos = lax.bitwise_xor(place, key // rows) * rows + lax.rem(key, rows)
    query_pos = place * rows + lax.broadcasted_iota(jnp.int32, shape, 0)
    return jnp.where((key_pos <= query_pos) & (key_pos < length), 0.0, MASKED).astype(F32)


def self_forward(
    scal, xall, wq, wk, wv, wo, wcq, gains, h1, q, k, v, att, lse, x1, h2, cq, bias
):
    rows = q.shape[0]
    key_count, width = xall.shape
    x = xall[...].astype(F32)
    h1[...] = (x * inv_rms(x) * gains[0:1]).astype(BF)
    q[...] = (nn(h1[0:rows], wq[...]) * SCALE).astype(BF)
    k[...] = nn(h1[...], wk[...]).astype(BF)
    v[...] = nn(h1[...], wv[...]).astype(BF)
    bias[...] = self_bias(scal[0], scal[1], rows, key_count)
    lane = lax.broadcasted_iota(jnp.int32, (rows, LANES), 1)
    stats = jnp.zeros((rows, LANES), F32)
    for quad in range(width // QUAD):
        cols = slice(quad * QUAD, (quad + 1) * QUAD)
        qq, kq, vq = q[:, cols], k[:, cols], v[:, cols]
        total = jnp.zeros((rows, QUAD), F32)
        for h in range(QUAD // HEAD):
            s = nt(only_head(qq, h), kq) + bias[...]
            m = jnp.max(s, axis=-1, keepdims=True)
            p = jnp.exp(s - m)
            z = jnp.sum(p, axis=-1, keepdims=True)
            o = nn(p.astype(BF), vq) * (1.0 / z)
            total = jnp.where(head_lane(rows) == h, o, total)
            stats = jnp.where(lane == quad * (QUAD // HEAD) + h, m + jnp.log(z), stats)
        att[:, cols] = total.astype(BF)
    lse[...] = stats
    mid = x[0:rows] + nn(att[...], wo[...])
    x1[...] = mid
    h2[...] = (mid * inv_rms(mid) * gains[1:2]).astype(BF)
    cq[...] = (nn(h2[...], wcq[...]) * SCALE).astype(BF)


def shift_in(x, groups):
    pad = jnp.zeros((groups * SPAN - x.shape[0], x.shape[1]), F32)
    return pltpu.roll(jnp.concatenate([x, pad], axis=0), 1, 0)


def shift_out(x, rows):
    return pltpu.roll(x, x.shape[0] - 1, 0)[0:rows]


def entry_rows(slots, group, n, own_rows):
    if group == 0:
        return pl.ds(own_rows + n * RET, RET)
    return pl.ds(pl.multiple_of(slots[(group - 1) * NEIGH + n] * RET, RET), RET)


def window(ref, places, cols):
    return jnp.concatenate([ref[at, cols] for at in places], axis=0)


def cross_forward(slots, nall, wck, wcv, cq, ck, cv, cout, qp, op):
    rows, width = cq.shape
    groups = rows // SPAN + 1
    own_rows = nall.shape[0] - NEIGH * RET
    ck[...] = nn(nall[...], wck[...]).astype(BF)
    cv[...] = nn(nall[...], wcv[...]).astype(BF)
    qp[...] = shift_in(cq[...].astype(F32), groups).astype(BF)
    for g in range(groups):
        places = [entry_rows(slots, g, n, own_rows) for n in range(NEIGH)]
        at = slice(g * SPAN, (g + 1) * SPAN)
        for quad in range(width // QUAD):
            cols = slice(quad * QUAD, (quad + 1) * QUAD)
            s = nt(by_heads(qp[at, cols]), window(ck, places, cols))
            p = jnp.exp(s - jnp.max(s, axis=-1, keepdims=True))
            p = p * (1.0 / jnp.sum(p, axis=-1, keepdims=True))
            op[at, cols] = from_heads(nn(p.astype(BF), window(cv, places, cols)))
    cout[...] = shift_out(op[...], rows).astype(BF)


def mlp_both(
    steps, x1, cout, dy, wco, win, wout, gains,
    out, grads, dx2, dcout, dgain, x2, h3, y, dh3, act,
):
    step = pl.program_id(0)

    @pl.when(step == 0)
    def _():
        x = x1[...] + nn(cout[...], wco[...])
        x2[...] = x
        h3[...] = (x * inv_rms(x) * gains[2:3]).astype(BF)
        y[...] = jnp.zeros_like(y)
        dh3[...] = jnp.zeros_like(dh3)

    @pl.when((step < steps - 1) & (lax.rem(step, 2) == 0))
    def _():
        u = nn(h3[...], win[...])
        t = jnp.tanh(GELU_C * (u + GELU_D * (u * u * u)))
        a = (0.5 * u * (1.0 + t)).astype(BF)
        act[...] = a
        y[...] += nn(a, wout[...])
        slope = 0.5 * (1.0 + t) + 0.5 * u * (1.0 - t * t) * (
            GELU_C * (1.0 + 3.0 * GELU_D * (u * u))
        )
        du = (nt(dy[...], wout[...]) * slope).astype(BF)
        dh3[...] += nt(du, win[...])
        grads[...] = tn(h3[...], du).astype(BF)

    @pl.when((step < steps - 1) & (lax.rem(step, 2) == 1))
    def _():
        grads[...] = tn(act[...], dy[...]).astype(BF)

    @pl.when(step == steps - 1)
    def _():
        x = x2[...]
        out[...] = (x + y[...]).astype(BF)
        dx, per_row = rms_back(x, gains[2:3], dh3[...])
        dx = dx + dy[...].astype(F32)
        dx2[...] = dx
        dc = dx.astype(BF)
        dgain[...] = column_sum(per_row, 2)
        grads[...] = tn(cout[...], dc).astype(BF)
        dcout[...] = nt(dc, wco[...]).astype(BF)


def cross_backward(slots, ck, cv, cq, dcout, wck, wcv, dck, dcv, dcq, gn, qp, dop, dqp):
    rows, width = cq.shape
    groups = rows // SPAN + 1
    own_rows = ck.shape[0] - NEIGH * RET
    qp[...] = shift_in(cq[...].astype(F32), groups).astype(BF)
    dop[...] = shift_in(dcout[...].astype(F32), groups).astype(BF)
    for g in range(groups):
        places = [entry_rows(slots, g, n, own_rows) for n in range(NEIGH)]
        at = slice(g * SPAN, (g + 1) * SPAN)
        for quad in range(width // QUAD):
            cols = slice(quad * QUAD, (quad + 1) * QUAD)
            keys = window(ck, places, cols)
            q4 = by_heads(qp[at, cols])
            do4 = by_heads(dop[at, cols])
            s = nt(q4, keys)
            p = jnp.exp(s - jnp.max(s, axis=-1, keepdims=True))
            p = p * (1.0 / jnp.sum(p, axis=-1, keepdims=True))
            dp = nt(do4, window(cv, places, cols))
            ds = (p * (dp - jnp.sum(p * dp, axis=-1, keepdims=True))).astype(BF)
            dqp[at, cols] = from_heads(nn(ds, keys)) * SCALE
            dk = tn(ds, q4).astype(BF)
            dv = tn(p.astype(BF), do4).astype(BF)
            for n in range(NEIGH):
                part = slice(n * RET, (n + 1) * RET)
                dck[places[n], cols] = dk[part]
                dcv[places[n], cols] = dv[part]
    dcq[...] = shift_out(dqp[...], rows).astype(BF)
    gn[...] = (nt(dck[...], wck[...]) + nt(dcv[...], wcv[...])).astype(BF)


def cross_weights(
    att, x1, h2, dx2, dcq, nall, dck, dcv, dgain, wo, wcq, gains, grads, dx1, datt, dgain_out
):
    width = x1.shape[1]

    def unit(u):
        return slice(u * width, (u + 1) * width)

    dx, per_row = rms_back(x1[...], gains[1:2], nt(dcq[...], wcq[...]))
    dx = dx + dx2[...]
    dx1[...] = dx
    da = dx.astype(BF)
    dgain_out[...] = dgain[...] + column_sum(per_row, 1)
    datt[...] = nt(da, wo[...]).astype(BF)
    grads[:, unit(0)] = tn(att[...], da).astype(BF)
    grads[:, unit(1)] = tn(h2[...], dcq[...]).astype(BF)
    grads[:, unit(2)] = tn(nall[...], dck[...]).astype(BF)
    grads[:, unit(3)] = tn(nall[...], dcv[...]).astype(BF)


def self_backward(
    scal, xall, h1, q, k, v, lse, datt, dgain, wq, wk, wv,
    grads, dh_own, dh_rest, dq, dk, dv, bias, st, gt,
):
    rows, width = q.shape
    key_count = k.shape[0]
    heads = QUAD // HEAD

    def unit(u):
        return slice(u * width, (u + 1) * width)

    bias[...] = self_bias(scal[0], scal[1], rows, key_count)
    lane = lax.broadcasted_iota(jnp.int32, (rows, LANES), 1)
    stats = lse[...]
    for quad in range(width // QUAD):
        cols = slice(quad * QUAD, (quad + 1) * QUAD)
        kq, vq = k[:, cols], v[:, cols]
        q4, da4 = by_heads(q[:, cols]), by_heads(datt[:, cols])
        for h in range(heads):
            at = slice(h * rows, (h + 1) * rows)
            level = jnp.sum(
                jnp.where(lane == quad * heads + h, stats, 0.0), axis=-1, keepdims=True
            )
            p = jnp.exp(nt(q4[at], kq) + bias[...] - level)
            dp = nt(da4[at], vq)
            ds = p * (dp - jnp.sum(p * dp, axis=-1, keepdims=True))
            st[at, :] = ds.astype(BF)
            gt[at, :] = p.astype(BF)
        dq[:, cols] = (from_heads(nn(st[...], kq)) * SCALE).astype(BF)
        dk[:, cols] = tn(st[...], q4).astype(BF)
        dv[:, cols] = tn(gt[...], da4).astype(BF)
    grads[:, unit(0)] = tn(h1[0:rows], dq[...]).astype(BF)
    grads[:, unit(1)] = tn(h1[...], dk[...]).astype(BF)
    grads[:, unit(2)] = tn(h1[...], dv[...]).astype(BF)
    gain_sum = dgain[...]
    for block in range(key_count // rows):
        at = slice(block * rows, (block + 1) * rows)
        part = nt(dk[at], wk[...]) + nt(dv[at], wv[...])
        if block == 0:
            part = part + nt(dq[...], wq[...])
            dh_own[...] = part
        else:
            dh_rest[(block - 1) * rows : block * rows] = part.astype(BF)
        x = xall[at].astype(F32)
        gain_sum = gain_sum + column_sum(part * (x * inv_rms(x)), 0)
    gain_sum = jnp.concatenate([gain_sum, jnp.zeros_like(gain_sum)], axis=1)
    grads[:, 3 * width :] = gain_sum.astype(BF)


def params():
    return pltpu.CompilerParams(vmem_limit_bytes=VMEM_LIMIT)


def scalar_spec():
    return pl.BlockSpec(memory_space=pltpu.SMEM)


def vmem_spec():
    return pl.BlockSpec(memory_space=pltpu.VMEM)


def unit_spec(width, u):
    return pl.BlockSpec((width, width), lambda i, u=u: (0, u))


def full_spec(shape):
    return pl.BlockSpec(shape, lambda i: (0,) * len(shape))


def sds(shape, dtype):
    return jax.ShapeDtypeStruct(shape, dtype)


def call(kernel, ins, outs, scratch, grid=(1,), flops=0):
    specs = [full_spec(a.shape) if s is None else s for a, s in ins]
    out_specs = [full_spec(o.shape) if s is None else s for o, s in outs]
    moved = sum(o.size * o.dtype.itemsize for o, _ in outs)
    return pl.pallas_call(
        kernel,
        grid=grid,
        in_specs=specs,
        out_specs=out_specs,
        out_shape=[o for o, _ in outs],
        scratch_shapes=scratch,
        compiler_params=params(),
        cost_estimate=pl.CostEstimate(flops=flops, bytes_accessed=2 * moved, transcendentals=0),
    )(*[a for a, _ in ins])


def split_four(x):
    rows, total = x.shape
    return x.reshape(rows, total // 4, 4).swapaxes(1, 2).reshape(rows, total)


def join_four(x):
    rows, total = x.shape
    return x.reshape(rows, 4, total // 4).swapaxes(1, 2).reshape(rows, total)


def exchange(x, by):
    peers = lax.axis_size("dp")
    return lax.ppermute(x, "dp", [(i, i ^ by) for i in range(peers)])


def shifted(x, by):
    peers = lax.axis_size("dp")
    return lax.ppermute(x, "dp", [(i, i + by) for i in range(peers) if 0 <= i + by < peers])


def scatter_sums(x, order):
    dp, nbr = lax.axis_size("dp"), lax.axis_size("nbr")
    y_count = 1 << ((nbr.bit_length() - 2) // 2)
    parts = {"x": dp // 2, "c": 2, "z": nbr // y_count, "y": y_count}
    strides = {"x": 2, "c": 1, "z": y_count, "y": 1}
    place = {}
    for name, count in parts.items():
        index = lax.axis_index("dp" if name in "xc" else "nbr")
        place[name] = lax.rem(index // strides[name], count)
    x = x.reshape(tuple(parts.values()) + (x.shape[0] // (dp * nbr), x.shape[1]))
    for name in "c" + order:
        axis, dim = ("dp" if name in "xc" else "nbr"), "xczy".index(name)
        total = lax.dynamic_slice_in_dim(x, place[name], 1, dim).astype(F32)
        for k in range(1, parts[name]):
            send = lax.dynamic_slice_in_dim(x, lax.bitwise_xor(place[name], k), 1, dim)
            pairs = [(i, i ^ (k * strides[name])) for i in range(lax.axis_size(axis))]
            total = total + lax.ppermute(send, axis, pairs).astype(F32)
        x = total.astype(BF)
    return x.reshape(x.shape[-2:])


def body(
    tokens,
    neighbours,
    lengths,
    slots,
    grad_out,
    w_query,
    w_key,
    w_value,
    w_attn_out,
    w_cross_query,
    w_cross_key,
    w_cross_value,
    w_cross_out,
    w_mlp_in,
    w_mlp_out,
    gain_attn,
    gain_cross,
    gain_mlp,
):
    peers = lax.axis_size("dp")
    _, rows, width = tokens.shape
    inner = w_mlp_in.shape[1]
    part = w_query.shape[0]
    key_count = rows * peers
    groups = rows // SPAN + 1
    halo = NEIGH * RET

    gains = jnp.stack([gain_attn, gain_cross, gain_mlp], axis=1)
    gains = jnp.pad(gains, ((0, 0), (0, LANES - 3)))
    shard = jnp.concatenate(
        [
            w_query,
            w_key,
            w_value,
            w_attn_out,
            w_cross_query,
            w_cross_key,
            w_cross_value,
            w_cross_out,
            split_four(w_mlp_in),
            w_mlp_out.reshape(part, inner),
            gains,
        ],
        axis=1,
    ).astype(BF)
    mats = lax.all_gather(shard, ("dp", "nbr"), axis=0, tiled=True)
    gain_rows = jnp.pad(mats[:, 8 * width + 2 * inner :][:, :3].astype(F32).T, ((0, 5), (0, 0)))

    def mat(u):
        return (mats, unit_spec(width, u))

    own_tokens = tokens[0]
    xall = jnp.concatenate([own_tokens] + [exchange(own_tokens, k) for k in range(1, peers)])
    entries = lax.all_to_all(neighbours, "nbr", split_axis=0, concat_axis=1, tiled=True)[0]
    own_rows = entries.shape[0]
    slot_list = slots.reshape(-1)
    last = [
        lax.dynamic_slice_in_dim(entries, slot_list[slot_list.shape[0] - NEIGH + n] * RET, RET)
        for n in range(NEIGH)
    ]
    behind = shifted(jnp.concatenate(last), 1)
    nall = jnp.concatenate([entries, behind])
    n_rows = own_rows + halo

    scal = jnp.stack([lax.axis_index("dp").astype(jnp.int32), lengths[0]])
    dy = grad_out[0]

    def low(*shape):
        return (sds(shape, BF), None)

    def wide(*shape):
        return (sds(shape, F32), None)

    h1, q, k, v, att, lse, x1, h2, cq = call(
        self_forward,
        [
            (scal, scalar_spec()), (xall, None), mat(U_Q), mat(U_K), mat(U_V), mat(U_O),
            mat(U_CQ), (gain_rows, None),
        ],
        [
            low(key_count, width), low(rows, width), low(key_count, width),
            low(key_count, width), low(rows, width), wide(rows, LANES), wide(rows, width),
            low(rows, width), low(rows, width),
        ],
        [pltpu.VMEM((rows, key_count), F32)],
    )
    ck, cv, cout = call(
        cross_forward,
        [(slot_list, scalar_spec()), (nall, None), mat(U_CK), mat(U_CV), (cq, None)],
        [low(n_rows, width), low(n_rows, width), low(rows, width)],
        [pltpu.VMEM((groups * SPAN, width), BF), pltpu.VMEM((groups * SPAN, width), F32)],
    )
    blocks = inner // width
    steps = 2 * blocks + 1

    def ahead(first):
        return pl.BlockSpec(
            (width, width), lambda i: (0, first + jnp.minimum(i // 2, blocks - 1))
        )

    out, mlp_grads, dx2, dcout, dgain = call(
        functools.partial(mlp_both, steps),
        [
            (x1, None), (cout, None), (dy, None), mat(U_CO), (mats, ahead(U_IN)),
            (mats, ahead(U_IN + blocks)), (gain_rows, None),
        ],
        [
            low(rows, width),
            (sds((width, steps * width), BF), pl.BlockSpec((width, width), lambda i: (0, i))),
            wide(rows, width), low(rows, width), wide(width, LANES),
        ],
        [
            pltpu.VMEM((rows, width), F32), pltpu.VMEM((rows, width), BF),
            pltpu.VMEM((rows, width), F32), pltpu.VMEM((rows, width), F32),
            pltpu.VMEM((rows, width), BF),
        ],
        grid=(steps,),
    )
    mlp_sum = lax.psum_scatter(mlp_grads, ("dp", "nbr"), scatter_dimension=0, tiled=True)

    dck, dcv, dcq, gn = call(
        cross_backward,
        [
            (slot_list, scalar_spec()), (ck, None), (cv, None), (cq, None), (dcout, None),
            mat(U_CK), mat(U_CV),
        ],
        [low(n_rows, width), low(n_rows, width), low(rows, width), low(n_rows, width)],
        [
            pltpu.VMEM((groups * SPAN, width), BF), pltpu.VMEM((groups * SPAN, width), BF),
            pltpu.VMEM((groups * SPAN, width), F32),
        ],
    )
    ahead_part = shifted(gn[own_rows:], -1)
    placed = gn[:own_rows].reshape(-1, RET, width)
    entry = jnp.arange(placed.shape[0], dtype=jnp.int32)[:, None, None]
    for n in range(NEIGH):
        extra = ahead_part[n * RET : (n + 1) * RET].astype(F32)
        here = entry == slot_list[slot_list.shape[0] - NEIGH + n]
        placed = placed + jnp.where(here, extra[None], 0.0)
    grad_nbr = lax.all_to_all(
        placed.astype(BF).reshape(1, own_rows, width),
        "nbr", split_axis=1, concat_axis=0, tiled=True,
    )

    branch_grads, dx1, datt, dgain = call(
        cross_weights,
        [
            (att, None), (x1, None), (h2, None), (dx2, None), (dcq, None), (nall, None),
            (dck, None), (dcv, None), (dgain, None), mat(U_O), mat(U_CQ), (gain_rows, None),
        ],
        [low(width, 4 * width), wide(rows, width), low(rows, width), wide(width, LANES)],
        [],
    )
    grads, dh_own, dh_rest = call(
        self_backward,
        [
            (scal, scalar_spec()), (xall, None), (h1, None), (q, None), (k, None), (v, None),
            (lse, None), (datt, None), (dgain, None), mat(U_Q), mat(U_K), mat(U_V),
        ],
        [low(width, 3 * width + 2 * LANES), wide(rows, width), low(key_count - rows, width)],
        [
            pltpu.VMEM((rows, width), BF), pltpu.VMEM((key_count, width), BF),
            pltpu.VMEM((key_count, width), BF), pltpu.VMEM((rows, key_count), F32),
            pltpu.VMEM((QUAD // HEAD * rows, key_count), BF),
            pltpu.VMEM((QUAD // HEAD * rows, key_count), BF),
        ],
    )
    branch_sum = scatter_sums(branch_grads, "yxz")
    rest_sum = scatter_sums(grads, "xyz")
    dh = dh_own
    for j in range(1, peers):
        dh = dh + exchange(dh_rest[(j - 1) * rows : j * rows], j).astype(F32)
    back, _ = rms_back(own_tokens.astype(F32), gain_rows[0:1], dh)
    grad_tokens = (dx1 + back).astype(BF)

    def of(sums, u):
        return sums[:, u * width : (u + 1) * width].astype(F32)

    pairs = mlp_sum[:, : 2 * inner].reshape(part, blocks, 2, width)
    return (
        out[None],
        grad_tokens[None],
        grad_nbr,
        of(rest_sum, 0),
        of(rest_sum, 1),
        of(rest_sum, 2),
        of(branch_sum, 0),
        of(branch_sum, 1),
        of(branch_sum, 2),
        of(branch_sum, 3),
        mlp_sum[:, 2 * inner :].astype(F32),
        join_four(pairs[:, :, 0].reshape(part, inner)).astype(F32),
        pairs[:, :, 1].reshape(4 * part, width).astype(F32),
        rest_sum[:, 3 * width].astype(F32),
        rest_sum[:, 3 * width + 1].astype(F32),
        rest_sum[:, 3 * width + 2].astype(F32),
    )


def solution(mesh):
    rows = P(("dp", "nbr"), None)
    vector = P(("dp", "nbr"))
    seq = P("nbr", "dp", None)
    nbr = P(None, ("dp", "nbr"), None)
    return jax.shard_map(
        body,
        mesh=mesh,
        in_specs=(seq, nbr, P("nbr"), seq, seq) + (rows,) * 10 + (vector,) * 3,
        out_specs=(seq, seq, nbr) + (rows,) * 10 + (vector,) * 3,
        check_vma=False,
    )
```

```python
import functools

import jax
import jax.numpy as jnp
from jax import lax
from jax.experimental import pallas as pl
from jax.experimental.pallas import tpu as pltpu
from jax.sharding import PartitionSpec as P

HEAD = 64
SPAN = 64
NEIGH = 2
RET = 128
QUAD = 256
LANES = 128

EPSILON = 1e-06
SCALE = 0.125
MASKED = -1e30
GELU_C = 0.7978845608
GELU_D = 0.044715

BF = jnp.bfloat16
F32 = jnp.float32
VMEM_LIMIT = 60 * 1024 * 1024

WHOLE_STEPS = 3
U_Q, U_K, U_V, U_O, U_CQ, U_CK, U_CV, U_CO, U_IN = range(9)


def nn(a, b):
    return lax.dot_general(a, b, (((1,), (0,)), ((), ())), preferred_element_type=F32)


def nt(a, b):
    return lax.dot_general(a, b, (((1,), (1,)), ((), ())), preferred_element_type=F32)


def tn(a, b):
    return lax.dot_general(a, b, (((0,), (0,)), ((), ())), preferred_element_type=F32)


def inv_rms(x):
    return lax.rsqrt(jnp.mean(x * x, axis=-1, keepdims=True) + EPSILON)


def rms_back(x, gain, dz):
    r = inv_rms(x)
    n = x * r
    dzg = dz * gain
    dx = r * (dzg - n * jnp.mean(dzg * n, axis=-1, keepdims=True))
    return dx, dz * n


def column_sum(values, column):
    rows = values.shape[0]
    pick = (lax.broadcasted_iota(jnp.int32, (rows, LANES), 1) == column).astype(BF)
    high = values.astype(BF)
    low = (values - high.astype(F32)).astype(BF)
    return tn(high, pick) + tn(low, pick)


def head_lane(rows):
    return lax.broadcasted_iota(jnp.int32, (rows, QUAD), 1) // HEAD


def only_head(x, h):
    return jnp.where(head_lane(x.shape[0]) == h, x, jnp.zeros_like(x))


def by_heads(x):
    return jnp.concatenate([only_head(x, h) for h in range(QUAD // HEAD)], axis=0)


def from_heads(x):
    rows = x.shape[0] // (QUAD // HEAD)
    lane = head_lane(rows)
    out = x[:rows]
    for h in range(1, QUAD // HEAD):
        out = jnp.where(lane == h, x[h * rows : (h + 1) * rows], out)
    return out


def self_bias(place, length, rows, key_count):
    shape = (rows, key_count)
    key = lax.broadcasted_iota(jnp.int32, shape, 1)
    key_pos = lax.bitwise_xor(place, key // rows) * rows + lax.rem(key, rows)
    query_pos = place * rows + lax.broadcasted_iota(jnp.int32, shape, 0)
    return jnp.where((key_pos <= query_pos) & (key_pos < length), 0.0, MASKED).astype(F32)


def self_forward(
    scal, xall, wq, wk, wv, wo, wcq, gains, h1, q, k, v, att, lse, x1, h2, cq, bias
):
    rows = q.shape[0]
    key_count, width = xall.shape
    x = xall[...].astype(F32)
    h1[...] = (x * inv_rms(x) * gains[0:1]).astype(BF)
    q[...] = (nn(h1[0:rows], wq[...]) * SCALE).astype(BF)
    k[...] = nn(h1[...], wk[...]).astype(BF)
    v[...] = nn(h1[...], wv[...]).astype(BF)
    bias[...] = self_bias(scal[0], scal[1], rows, key_count)
    lane = lax.broadcasted_iota(jnp.int32, (rows, LANES), 1)
    stats = jnp.zeros((rows, LANES), F32)
    for quad in range(width // QUAD):
        cols = slice(quad * QUAD, (quad + 1) * QUAD)
        qq, kq, vq = q[:, cols], k[:, cols], v[:, cols]
        total = jnp.zeros((rows, QUAD), F32)
        for h in range(QUAD // HEAD):
            s = nt(only_head(qq, h), kq) + bias[...]
            m = jnp.max(s, axis=-1, keepdims=True)
            p = jnp.exp(s - m)
            z = jnp.sum(p, axis=-1, keepdims=True)
            o = nn(p.astype(BF), vq) * (1.0 / z)
            total = jnp.where(head_lane(rows) == h, o, total)
            stats = jnp.where(lane == quad * (QUAD // HEAD) + h, m + jnp.log(z), stats)
        att[:, cols] = total.astype(BF)
    lse[...] = stats
    mid = x[0:rows] + nn(att[...], wo[...])
    x1[...] = mid
    h2[...] = (mid * inv_rms(mid) * gains[1:2]).astype(BF)
    cq[...] = (nn(h2[...], wcq[...]) * SCALE).astype(BF)


def shift_in(x, groups):
    pad = jnp.zeros((groups * SPAN - x.shape[0], x.shape[1]), F32)
    return pltpu.roll(jnp.concatenate([x, pad], axis=0), 1, 0)


def shift_out(x, rows):
    return pltpu.roll(x, x.shape[0] - 1, 0)[0:rows]


def entry_rows(slots, group, n, own_rows):
    if group == 0:
        return pl.ds(own_rows + n * RET, RET)
    return pl.ds(pl.multiple_of(slots[(group - 1) * NEIGH + n] * RET, RET), RET)


def window(ref, places, cols):
    return jnp.concatenate([ref[at, cols] for at in places], axis=0)


def cross_forward(slots, nall, wck, wcv, cq, ck, cv, cout, qp, op):
    rows, width = cq.shape
    groups = rows // SPAN + 1
    own_rows = nall.shape[0] - NEIGH * RET
    ck[...] = nn(nall[...], wck[...]).astype(BF)
    cv[...] = nn(nall[...], wcv[...]).astype(BF)
    qp[...] = shift_in(cq[...].astype(F32), groups).astype(BF)
    for g in range(groups):
        places = [entry_rows(slots, g, n, own_rows) for n in range(NEIGH)]
        at = slice(g * SPAN, (g + 1) * SPAN)
        for quad in range(width // QUAD):
            cols = slice(quad * QUAD, (quad + 1) * QUAD)
            s = nt(by_heads(qp[at, cols]), window(ck, places, cols))
            p = jnp.exp(s - jnp.max(s, axis=-1, keepdims=True))
            p = p * (1.0 / jnp.sum(p, axis=-1, keepdims=True))
            op[at, cols] = from_heads(nn(p.astype(BF), window(cv, places, cols)))
    cout[...] = shift_out(op[...], rows).astype(BF)


def part_ways(keep, send, cols, total, core, chips):
    rows = total.shape[0] // (2 * chips)
    for x in range(chips):
        first = total[2 * x * rows : (2 * x + 1) * rows]
        second = total[(2 * x + 1) * rows : (2 * x + 2) * rows]
        at = slice(x * rows, (x + 1) * rows)
        keep[at, cols] = jnp.where(core == 0, first, second).astype(BF)
        send[at, cols] = jnp.where(core == 0, second, first).astype(BF)


def mlp_both(
    steps, chips, scal, x1, cout, dy, wco, win, wout, gains,
    out, whole, keep, send, dx2, dcout, dgain, x2, h3, y, dh3,
):
    step = pl.program_id(0)
    width = x1.shape[1]

    @pl.when(step == 0)
    def _():
        x = x1[...] + nn(cout[...], wco[...])
        x2[...] = x
        h3[...] = (x * inv_rms(x) * gains[2:3]).astype(BF)
        y[...] = jnp.zeros_like(y)
        dh3[...] = jnp.zeros_like(dh3)

    u = nn(h3[...], win[...])
    t = jnp.tanh(GELU_C * (u + GELU_D * (u * u * u)))
    act = (0.5 * u * (1.0 + t)).astype(BF)
    y[...] += nn(act, wout[...])
    slope = 0.5 * (1.0 + t) + 0.5 * u * (1.0 - t * t) * (GELU_C * (1.0 + 3.0 * GELU_D * (u * u)))
    du = (nt(dy[...], wout[...]) * slope).astype(BF)
    dh3[...] += nt(du, win[...])

    @pl.when(step < WHOLE_STEPS)
    def _():
        whole[:, :width] = tn(h3[...], du).astype(BF)
        whole[:, width:] = tn(act, dy[...]).astype(BF)

    @pl.when(step >= WHOLE_STEPS)
    def _():
        part_ways(keep, send, slice(0, width), tn(h3[...], du), scal[2], chips)
        part_ways(keep, send, slice(width, None), tn(act, dy[...]), scal[2], chips)

    @pl.when(step == steps - 1)
    def _():
        x = x2[...]
        out[...] = (x + y[...]).astype(BF)
        dx, per_row = rms_back(x, gains[2:3], dh3[...])
        dx = dx + dy[...].astype(F32)
        dx2[...] = dx
        dgain[...] = column_sum(per_row, 2)
        dcout[...] = nt(dx.astype(BF), wco[...]).astype(BF)


def cross_backward(slots, ck, cv, cq, dcout, wck, wcv, dck, dcv, dcq, gn, qp, dop, dqp):
    rows, width = cq.shape
    groups = rows // SPAN + 1
    own_rows = ck.shape[0] - NEIGH * RET
    qp[...] = shift_in(cq[...].astype(F32), groups).astype(BF)
    dop[...] = shift_in(dcout[...].astype(F32), groups).astype(BF)
    for g in range(groups):
        places = [entry_rows(slots, g, n, own_rows) for n in range(NEIGH)]
        at = slice(g * SPAN, (g + 1) * SPAN)
        for quad in range(width // QUAD):
            cols = slice(quad * QUAD, (quad + 1) * QUAD)
            keys = window(ck, places, cols)
            q4 = by_heads(qp[at, cols])
            do4 = by_heads(dop[at, cols])
            s = nt(q4, keys)
            p = jnp.exp(s - jnp.max(s, axis=-1, keepdims=True))
            p = p * (1.0 / jnp.sum(p, axis=-1, keepdims=True))
            dp = nt(do4, window(cv, places, cols))
            ds = (p * (dp - jnp.sum(p * dp, axis=-1, keepdims=True))).astype(BF)
            dqp[at, cols] = from_heads(nn(ds, keys)) * SCALE
            dk = tn(ds, q4).astype(BF)
            dv = tn(p.astype(BF), do4).astype(BF)
            for n in range(NEIGH):
                part = slice(n * RET, (n + 1) * RET)
                dck[places[n], cols] = dk[part]
                dcv[places[n], cols] = dv[part]
    dcq[...] = shift_out(dqp[...], rows).astype(BF)
    gn[...] = (nt(dck[...], wck[...]) + nt(dcv[...], wcv[...])).astype(BF)


def branch_backward(
    chips, scal, att, x1, h2, dx2, dcq, nall, dck, dcv, dgain, cout, q, k, v, lse,
    wo, wcq, gains,
    keep, send, dx1, dgain_out, dq, dk, dv, bias, st, gt, datt,
):
    rows, width = x1.shape

    def put(u, total):
        part_ways(keep, send, slice(u * width, (u + 1) * width), total, scal[2], chips)

    dx, per_row = rms_back(x1[...], gains[1:2], nt(dcq[...], wcq[...]))
    dx = dx + dx2[...]
    dx1[...] = dx
    da = dx.astype(BF)
    dgain_out[...] = dgain[...] + column_sum(per_row, 1)
    datt[...] = nt(da, wo[...]).astype(BF)
    put(0, tn(att[...], da))
    put(1, tn(h2[...], dcq[...]))
    put(2, tn(nall[...], dck[...]))
    put(3, tn(nall[...], dcv[...]))
    put(4, tn(cout[...], dx2[...].astype(BF)))
    heads = QUAD // HEAD
    bias[...] = self_bias(scal[0], scal[1], rows, k.shape[0])
    lane = lax.broadcasted_iota(jnp.int32, (rows, LANES), 1)
    stats = lse[...]
    for quad in range(width // QUAD):
        cols = slice(quad * QUAD, (quad + 1) * QUAD)
        kq, vq = k[:, cols], v[:, cols]
        q4, da4 = by_heads(q[:, cols]), by_heads(datt[:, cols])
        for h in range(heads):
            at = slice(h * rows, (h + 1) * rows)
            level = jnp.sum(
                jnp.where(lane == quad * heads + h, stats, 0.0), axis=-1, keepdims=True
            )
            p = jnp.exp(nt(q4[at], kq) + bias[...] - level)
            dp = nt(da4[at], vq)
            ds = p * (dp - jnp.sum(p * dp, axis=-1, keepdims=True))
            st[at, :] = ds.astype(BF)
            gt[at, :] = p.astype(BF)
        dq[:, cols] = (from_heads(nn(st[...], kq)) * SCALE).astype(BF)
        dk[:, cols] = tn(st[...], q4).astype(BF)
        dv[:, cols] = tn(gt[...], da4).astype(BF)


def self_weights(chips, scal, h1, dq, dk, dv, dgain, wq, wk, wv, gain_cols, keep, send):
    rows, width = dq.shape
    products = jnp.zeros((width, 1), F32)
    for u, (rows_of, grad, w) in enumerate(((rows, dq, wq), (None, dk, wk), (None, dv, wv))):
        total = tn(h1[0:rows_of], grad[...])
        cols = slice(u * width, (u + 1) * width)
        part_ways(keep, send, cols, total, scal[2], chips)
        products = products + jnp.sum(total * w[...].astype(F32), axis=-1, keepdims=True)
    first = products / gain_cols[:, 0:1].astype(F32)
    lane = lax.broadcasted_iota(jnp.int32, (width, LANES), 1)
    total = jnp.where(lane == 0, first, dgain[...])
    total = jnp.concatenate([total, jnp.zeros_like(total)], axis=1)
    part_ways(keep, send, slice(3 * width, None), total, scal[2], chips)


def self_inputs(peers, dq, dk, dv, wq, wk, wv, keep, send):
    rows = dq.shape[0]
    for block in range(peers):
        at = slice(block * rows, (block + 1) * rows)
        part = nt(dk[at], wk[...]) + nt(dv[at], wv[...])
        if block == 0:
            part = part + nt(dq[...], wq[...])
        to = slice(block // 2 * rows, (block // 2 + 1) * rows)
        if block % 2 == 0:
            keep[to] = part
        else:
            send[to] = part.astype(BF)


def fold_kernel(places, count, scal, *refs):
    ins, outs = refs[: 2 * count], refs[2 * count :]
    start = 0
    for i in range(count):
        kept, came = ins[2 * i], ins[2 * i + 1]
        cols = slice(start, start + kept.shape[-1])
        start = start + kept.shape[-1]
        for k in range(places):
            at = pl.ds(lax.bitwise_xor(scal[0], k), 1)
            total = kept[:, at].astype(F32) + came[:, at].astype(F32)
            outs[k][:, :, cols] = total[:, 0].astype(BF)


def last_kernel(count, *refs):
    total = refs[0][...].astype(F32)
    for came in refs[1:count]:
        total = total + came[...].astype(F32)
    start = 0
    for out in refs[count:]:
        out[...] = total[:, start : start + out.shape[1]]
        start = start + out.shape[1]


def params():
    return pltpu.CompilerParams(vmem_limit_bytes=VMEM_LIMIT)


def scalar_spec():
    return pl.BlockSpec(memory_space=pltpu.SMEM)


def vmem_spec():
    return pl.BlockSpec(memory_space=pltpu.VMEM)


def unit_spec(width, u):
    return pl.BlockSpec((width, width), lambda i, u=u: (0, u))


def full_spec(shape):
    return pl.BlockSpec(shape, lambda i: (0,) * len(shape))


def sds(shape, dtype):
    return jax.ShapeDtypeStruct(shape, dtype)


def call(kernel, ins, outs, scratch, grid=(1,), us=10, after=()):
    specs = [full_spec(a.shape) if s is None else s for a, s in ins]
    specs = specs + [pl.BlockSpec(memory_space=pl.ANY)] * len(after)
    out_specs = [full_spec(o.shape) if s is None else s for o, s in outs]
    moved = sum(o.size * o.dtype.itemsize for o, _ in outs)

    def wrapped(*refs):
        kernel(*refs[: len(ins)], *refs[len(ins) + len(after) :])

    return pl.pallas_call(
        wrapped,
        grid=grid,
        in_specs=specs,
        out_specs=out_specs,
        out_shape=[o for o, _ in outs],
        scratch_shapes=scratch,
        compiler_params=params(),
        cost_estimate=pl.CostEstimate(
            flops=int(us * 1.1e9), bytes_accessed=2 * moved, transcendentals=0
        ),
    )(*[a for a, _ in ins], *after)


def split_four(x):
    rows, total = x.shape
    return x.reshape(rows, total // 4, 4).swapaxes(1, 2).reshape(rows, total)


def join_four(x):
    rows, total = x.shape
    return x.reshape(rows, 4, total // 4).swapaxes(1, 2).reshape(rows, total)


def exchange(x, by):
    peers = lax.axis_size("dp")
    return lax.ppermute(x, "dp", [(i, i ^ by) for i in range(peers)])


def shifted(x, by):
    peers = lax.axis_size("dp")
    return lax.ppermute(x, "dp", [(i, i + by) for i in range(peers) if 0 <= i + by < peers])


def axes_of():
    dp, nbr = lax.axis_size("dp"), lax.axis_size("nbr")
    y_count = 1 << ((nbr.bit_length() - 2) // 2)
    parts = {"x": dp // 2, "c": 2, "z": nbr // y_count, "y": y_count}
    strides = {"x": 2, "c": 1, "z": y_count, "y": 1}
    return parts, strides


def place_on(name):
    parts, strides = axes_of()
    return lax.rem(lax.axis_index("dp" if name in "xc" else "nbr") // strides[name], parts[name])


def pass_on(x, name, k=1):
    _, strides = axes_of()
    axis = "dp" if name in "xc" else "nbr"
    pairs = [(i, i ^ (k * strides[name])) for i in range(lax.axis_size(axis))]
    return lax.ppermute(x, axis, pairs)


def column_block(cols):
    return max(c for c in range(LANES, min(cols, 1024) + 1, LANES) if cols % c == 0)


def fold(pairs, left, name):
    parts, _ = axes_of()
    before, after = left.split(name)
    own = pairs[0][0].shape[0]
    for axis in left:
        own = own // parts[axis]
    lead, inner, places = 1, own, parts[name]
    for axis in before:
        lead = lead * parts[axis]
    for axis in after:
        inner = inner * parts[axis]
    arrays = [x.reshape(lead, places, inner, x.shape[1]) for pair in pairs for x in pair]
    cols = sum(pair[0].shape[1] for pair in pairs)
    block = column_block(cols) if len(pairs) == 1 else cols

    def spec(x):
        width = block if len(pairs) == 1 else x.shape[-1]
        return pl.BlockSpec(x.shape[:-1] + (width,), lambda i: (0,) * (x.ndim - 1) + (i,))

    out = sds((lead, inner, cols), BF)
    outs = call(
        functools.partial(fold_kernel, places, len(pairs)),
        [(place_on(name).reshape(1).astype(jnp.int32), scalar_spec())]
        + [(x, spec(x)) for x in arrays],
        [(out, pl.BlockSpec((lead, inner, block), lambda i: (0, 0, i)))] * places,
        [],
        grid=(cols // block,),
        us=3,
    )
    return [x.reshape(lead * inner, cols) for x in outs]


def fold_last(parts_of, widths):
    kept, sends = parts_of[0], parts_of[1:]
    came = [pass_on(x, "z", k + 1) for k, x in enumerate(sends)]
    return call(
        functools.partial(last_kernel, 1 + len(came)),
        [(x, None) for x in [kept] + came],
        [(sds((kept.shape[0], w), F32), None) for w in widths],
        [],
        us=2,
    )


def body(
    tokens,
    neighbours,
    lengths,
    slots,
    grad_out,
    w_query,
    w_key,
    w_value,
    w_attn_out,
    w_cross_query,
    w_cross_key,
    w_cross_value,
    w_cross_out,
    w_mlp_in,
    w_mlp_out,
    gain_attn,
    gain_cross,
    gain_mlp,
):
    peers = lax.axis_size("dp")
    _, rows, width = tokens.shape
    inner = w_mlp_in.shape[1]
    part = w_query.shape[0]
    key_count = rows * peers
    groups = rows // SPAN + 1
    halo = NEIGH * RET

    gains = jnp.stack([gain_attn, gain_cross, gain_mlp], axis=1)
    gains = jnp.pad(gains, ((0, 0), (0, LANES - 3)))
    shard = jnp.concatenate(
        [
            w_query,
            w_key,
            w_value,
            w_attn_out,
            w_cross_query,
            w_cross_key,
            w_cross_value,
            w_cross_out,
            split_four(w_mlp_in),
            w_mlp_out.reshape(part, inner),
            gains,
        ],
        axis=1,
    ).astype(BF)
    mats = lax.all_gather(shard, ("dp", "nbr"), axis=0, tiled=True)
    gain_rows = jnp.pad(mats[:, 8 * width + 2 * inner :][:, :3].astype(F32).T, ((0, 5), (0, 0)))

    def mat(u):
        return (mats, unit_spec(width, u))

    own_tokens = tokens[0]
    xall = jnp.concatenate([own_tokens] + [exchange(own_tokens, k) for k in range(1, peers)])
    entries = lax.all_to_all(neighbours, "nbr", split_axis=0, concat_axis=1, tiled=True)[0]
    own_rows = entries.shape[0]
    slot_list = slots.reshape(-1)
    last = [
        lax.dynamic_slice_in_dim(entries, slot_list[slot_list.shape[0] - NEIGH + n] * RET, RET)
        for n in range(NEIGH)
    ]
    behind = shifted(jnp.concatenate(last), 1)
    nall = jnp.concatenate([entries, behind])
    n_rows = own_rows + halo

    chips = peers // 2
    scal = jnp.stack(
        [lax.axis_index("dp").astype(jnp.int32), lengths[0], place_on("c").astype(jnp.int32)]
    )
    dy = grad_out[0]

    def low(*shape):
        return (sds(shape, BF), None)

    def wide(*shape):
        return (sds(shape, F32), None)

    h1, q, k, v, att, lse, x1, h2, cq = call(
        self_forward,
        [
            (scal, scalar_spec()), (xall, None), mat(U_Q), mat(U_K), mat(U_V), mat(U_O),
            mat(U_CQ), (gain_rows, None),
        ],
        [
            low(key_count, width), low(rows, width), low(key_count, width),
            low(key_count, width), low(rows, width), wide(rows, LANES), wide(rows, width),
            low(rows, width), low(rows, width),
        ],
        [pltpu.VMEM((rows, key_count), F32)],
        us=13,
    )
    ck, cv, cout = call(
        cross_forward,
        [(slot_list, scalar_spec()), (nall, None), mat(U_CK), mat(U_CV), (cq, None)],
        [low(n_rows, width), low(n_rows, width), low(rows, width)],
        [pltpu.VMEM((groups * SPAN, width), BF), pltpu.VMEM((groups * SPAN, width), F32)],
    )
    blocks = inner // width
    steps = blocks
    half = width // 2
    wide_block = 2 * width
    n_part = blocks - WHOLE_STEPS

    def ahead(first):
        return pl.BlockSpec((width, width), lambda i: (0, first + i))

    parted = (
        sds((half, n_part * wide_block), BF),
        pl.BlockSpec((half, wide_block), lambda i: (0, jnp.maximum(i - WHOLE_STEPS, 0))),
    )
    out, whole, mlp, mlp_send, dx2, dcout, dgain = call(
        functools.partial(mlp_both, steps, chips),
        [
            (scal, scalar_spec()), (x1, None), (cout, None), (dy, None), mat(U_CO),
            (mats, ahead(U_IN)), (mats, ahead(U_IN + blocks)), (gain_rows, None),
        ],
        [
            low(rows, width),
            (
                sds((width, WHOLE_STEPS * wide_block), BF),
                pl.BlockSpec((width, wide_block), lambda i: (0, jnp.minimum(i, WHOLE_STEPS - 1))),
            ),
            parted, parted,
            wide(rows, width), low(rows, width), wide(width, LANES),
        ],
        [
            pltpu.VMEM((rows, width), F32), pltpu.VMEM((rows, width), BF),
            pltpu.VMEM((rows, width), F32), pltpu.VMEM((rows, width), F32),
        ],
        grid=(steps,), us=16,
    )
    whole_sum = lax.psum_scatter(whole, ("dp", "nbr"), scatter_dimension=0, tiled=True)
    mlp = fold([(mlp, pass_on(mlp_send, "c"))], "xzy", "x")

    dck, dcv, dcq, gn = call(
        cross_backward,
        [
            (slot_list, scalar_spec()), (ck, None), (cv, None), (cq, None), (dcout, None),
            mat(U_CK), mat(U_CV),
        ],
        [low(n_rows, width), low(n_rows, width), low(rows, width), low(n_rows, width)],
        [
            pltpu.VMEM((groups * SPAN, width), BF), pltpu.VMEM((groups * SPAN, width), BF),
            pltpu.VMEM((groups * SPAN, width), F32),
        ],
        us=16,
    )
    ahead_part = shifted(gn[own_rows:], -1)
    placed = gn[:own_rows].reshape(-1, RET, width)
    entry = jnp.arange(placed.shape[0], dtype=jnp.int32)[:, None, None]
    for n in range(NEIGH):
        extra = ahead_part[n * RET : (n + 1) * RET].astype(F32)
        here = entry == slot_list[slot_list.shape[0] - NEIGH + n]
        placed = placed + jnp.where(here, extra[None], 0.0)
    placed = placed.astype(BF).reshape(neighbours.shape)
    grad_nbr = lax.all_to_all(placed, "nbr", split_axis=0, concat_axis=0, tiled=True)

    branch, branch_send, dx1, dgain, dq, dk, dv = call(
        functools.partial(branch_backward, chips),
        [
            (scal, scalar_spec()), (att, None), (x1, None), (h2, None), (dx2, None),
            (dcq, None), (nall, None), (dck, None), (dcv, None), (dgain, None), (cout, None),
            (q, None), (k, None), (v, None), (lse, None), mat(U_O), mat(U_CQ),
            (gain_rows, None),
        ],
        [
            low(half, 5 * width), low(half, 5 * width), wide(rows, width), wide(width, LANES),
            low(rows, width), low(key_count, width), low(key_count, width),
        ],
        [
            pltpu.VMEM((rows, key_count), F32),
            pltpu.VMEM((QUAD // HEAD * rows, key_count), BF),
            pltpu.VMEM((QUAD // HEAD * rows, key_count), BF),
            pltpu.VMEM((rows, width), BF),
        ],
        us=26,
        after=[placed, mlp[1]],
    )
    rest_cols = 3 * width + 2 * LANES
    rest, rest_send = call(
        functools.partial(self_weights, chips),
        [
            (scal, scalar_spec()), (h1, None), (dq, None), (dk, None), (dv, None),
            (dgain, None), mat(U_Q), mat(U_K), mat(U_V),
            (mats, pl.BlockSpec((width, LANES), lambda i: (0, (8 * width + 2 * inner) // LANES))),
        ],
        [low(half, rest_cols), low(half, rest_cols)],
        [],
        us=6,
    )
    mlp = fold([(mlp[0], pass_on(mlp[1], "x"))], "zy", "y")
    branch = fold([(branch, pass_on(branch_send, "c"))], "xzy", "x")
    dh, dh_send = call(
        functools.partial(self_inputs, peers),
        [(dq, None), (dk, None), (dv, None), mat(U_Q), mat(U_K), mat(U_V)],
        [wide(key_count // 2, width), low(key_count // 2, width)],
        [],
        us=6,
        after=[mlp[1], branch[1]],
    )
    rest = fold([(rest, pass_on(rest_send, "c"))], "xzy", "y")
    branch = fold([(branch[0], pass_on(branch[1], "x"))], "zy", "y")
    mlp = fold([(mlp[0], pass_on(mlp[1], "y"))], "z", "z")
    part_sum = fold_last(mlp, [n_part * wide_block])[0]
    rest = fold([(rest[0], pass_on(rest[1], "y"))], "xz", "x")
    tail = fold(
        [(branch[0], pass_on(branch[1], "y")), (rest[0], pass_on(rest[1], "x"))], "z", "z"
    )
    g_o, g_cq, g_ck, g_cv, g_co, g_q, g_k, g_v, g_gains = fold_last(
        tail, [width] * 8 + [2 * LANES]
    )
    sums = jnp.concatenate([whole_sum.astype(F32), part_sum], axis=1)
    sums = sums.reshape(part, blocks, 2, width)

    dh = (dh + exchange(dh_send, 1).astype(F32)).reshape(-1, rows, width)
    by = 2
    while by < peers:
        dh = dh[0::2] + exchange(dh[1::2].astype(BF), by).astype(F32)
        by = 2 * by
    dh = dh[0]
    back, _ = rms_back(own_tokens.astype(F32), gain_rows[0:1], dh)
    grad_tokens = (dx1 + back).astype(BF)

    return (
        out[None],
        grad_tokens[None],
        grad_nbr,
        g_q,
        g_k,
        g_v,
        g_o,
        g_cq,
        g_ck,
        g_cv,
        g_co,
        join_four(sums[:, :, 0].reshape(part, inner)),
        sums[:, :, 1].reshape(blocks * part, width),
        g_gains[:, 0],
        g_gains[:, 1],
        g_gains[:, 2],
    )


def solution(mesh):
    rows = P(("dp", "nbr"), None)
    vector = P(("dp", "nbr"))
    seq = P("nbr", "dp", None)
    nbr = P(None, ("dp", "nbr"), None)
    return jax.shard_map(
        body,
        mesh=mesh,
        in_specs=(seq, nbr, P("nbr"), seq, seq) + (rows,) * 10 + (vector,) * 3,
        out_specs=(seq, seq, nbr) + (rows,) * 10 + (vector,) * 3,
        check_vma=False,
    )
```

```python
import functools

import jax
import jax.numpy as jnp
from jax import lax
from jax.experimental import pallas as pl
from jax.experimental.pallas import tpu as pltpu
from jax.sharding import PartitionSpec as P

HEAD = 64
SPAN = 64
NEIGH = 2
RET = 128
QUAD = 256
LANES = 128

EPSILON = 1e-06
SCALE = 0.125
MASKED = -1e30
GELU_C = 0.7978845608
GELU_D = 0.044715

BF = jnp.bfloat16
F32 = jnp.float32
VMEM_LIMIT = 60 * 1024 * 1024

WHOLE_STEPS = 3
U_Q, U_K, U_V, U_O, U_CQ, U_CK, U_CV, U_CO, U_IN = range(9)


def nn(a, b):
    return lax.dot_general(a, b, (((1,), (0,)), ((), ())), preferred_element_type=F32)


def nt(a, b):
    return lax.dot_general(a, b, (((1,), (1,)), ((), ())), preferred_element_type=F32)


def tn(a, b):
    return lax.dot_general(a, b, (((0,), (0,)), ((), ())), preferred_element_type=F32)


def inv_rms(x):
    return lax.rsqrt(jnp.mean(x * x, axis=-1, keepdims=True) + EPSILON)


def rms_back(x, gain, dz):
    r = inv_rms(x)
    n = x * r
    dzg = dz * gain
    dx = r * (dzg - n * jnp.mean(dzg * n, axis=-1, keepdims=True))
    return dx, dz * n


def column_sum(values, column):
    rows = values.shape[0]
    pick = (lax.broadcasted_iota(jnp.int32, (rows, LANES), 1) == column).astype(BF)
    high = values.astype(BF)
    low = (values - high.astype(F32)).astype(BF)
    return tn(high, pick) + tn(low, pick)


def head_lane(rows):
    return lax.broadcasted_iota(jnp.int32, (rows, QUAD), 1) // HEAD


def only_head(x, h):
    return jnp.where(head_lane(x.shape[0]) == h, x, jnp.zeros_like(x))


def by_heads(x):
    return jnp.concatenate([only_head(x, h) for h in range(QUAD // HEAD)], axis=0)


def from_heads(x):
    rows = x.shape[0] // (QUAD // HEAD)
    lane = head_lane(rows)
    out = x[:rows]
    for h in range(1, QUAD // HEAD):
        out = jnp.where(lane == h, x[h * rows : (h + 1) * rows], out)
    return out


def self_bias(place, length, rows, key_count):
    shape = (rows, key_count)
    key = lax.broadcasted_iota(jnp.int32, shape, 1)
    key_pos = lax.bitwise_xor(place, key // rows) * rows + lax.rem(key, rows)
    query_pos = place * rows + lax.broadcasted_iota(jnp.int32, shape, 0)
    return jnp.where((key_pos <= query_pos) & (key_pos < length), 0.0, MASKED).astype(F32)


def self_forward(
    scal, xall, wq, wk, wv, wo, wcq, gains, h1, q, k, v, att, lse, x1, h2, cq, bias
):
    rows = q.shape[0]
    key_count, width = xall.shape
    x = xall[...].astype(F32)
    h1[...] = (x * inv_rms(x) * gains[0:1]).astype(BF)
    q[...] = (nn(h1[0:rows], wq[...]) * SCALE).astype(BF)
    k[...] = nn(h1[...], wk[...]).astype(BF)
    v[...] = nn(h1[...], wv[...]).astype(BF)
    bias[...] = self_bias(scal[0], scal[1], rows, key_count)
    lane = lax.broadcasted_iota(jnp.int32, (rows, LANES), 1)
    stats = jnp.zeros((rows, LANES), F32)
    for quad in range(width // QUAD):
        cols = slice(quad * QUAD, (quad + 1) * QUAD)
        qq, kq, vq = q[:, cols], k[:, cols], v[:, cols]
        total = jnp.zeros((rows, QUAD), F32)
        for h in range(QUAD // HEAD):
            s = nt(only_head(qq, h), kq) + bias[...]
            m = jnp.max(s, axis=-1, keepdims=True)
            p = jnp.exp(s - m)
            z = jnp.sum(p, axis=-1, keepdims=True)
            o = nn(p.astype(BF), vq) * (1.0 / z)
            total = jnp.where(head_lane(rows) == h, o, total)
            stats = jnp.where(lane == quad * (QUAD // HEAD) + h, m + jnp.log(z), stats)
        att[:, cols] = total.astype(BF)
    lse[...] = stats
    mid = x[0:rows] + nn(att[...], wo[...])
    x1[...] = mid
    h2[...] = (mid * inv_rms(mid) * gains[1:2]).astype(BF)
    cq[...] = (nn(h2[...], wcq[...]) * SCALE).astype(BF)


def shift_in(x, groups):
    pad = jnp.zeros((groups * SPAN - x.shape[0], x.shape[1]), F32)
    return pltpu.roll(jnp.concatenate([x, pad], axis=0), 1, 0)


def shift_out(x, rows):
    return pltpu.roll(x, x.shape[0] - 1, 0)[0:rows]


def entry_rows(slots, group, n, own_rows):
    if group == 0:
        return pl.ds(own_rows + n * RET, RET)
    return pl.ds(pl.multiple_of(slots[(group - 1) * NEIGH + n] * RET, RET), RET)


def window(ref, places, cols):
    return jnp.concatenate([ref[at, cols] for at in places], axis=0)


def cross_forward(slots, nall, wck, wcv, cq, ck, cv, cout, qp, op):
    rows, width = cq.shape
    groups = rows // SPAN + 1
    own_rows = nall.shape[0] - NEIGH * RET
    ck[...] = nn(nall[...], wck[...]).astype(BF)
    cv[...] = nn(nall[...], wcv[...]).astype(BF)
    qp[...] = shift_in(cq[...].astype(F32), groups).astype(BF)
    for g in range(groups):
        places = [entry_rows(slots, g, n, own_rows) for n in range(NEIGH)]
        at = slice(g * SPAN, (g + 1) * SPAN)
        for quad in range(width // QUAD):
            cols = slice(quad * QUAD, (quad + 1) * QUAD)
            s = nt(by_heads(qp[at, cols]), window(ck, places, cols))
            p = jnp.exp(s - jnp.max(s, axis=-1, keepdims=True))
            p = p * (1.0 / jnp.sum(p, axis=-1, keepdims=True))
            op[at, cols] = from_heads(nn(p.astype(BF), window(cv, places, cols)))
    cout[...] = shift_out(op[...], rows).astype(BF)


def part_ways(keep, send, cols, total, core, chips):
    rows = total.shape[0] // (2 * chips)
    for x in range(chips):
        first = total[2 * x * rows : (2 * x + 1) * rows]
        second = total[(2 * x + 1) * rows : (2 * x + 2) * rows]
        at = slice(x * rows, (x + 1) * rows)
        keep[at, cols] = jnp.where(core == 0, first, second).astype(BF)
        send[at, cols] = jnp.where(core == 0, second, first).astype(BF)


def mlp_both(
    steps, chips, scal, x1, cout, dy, wco, win, wout, gains,
    out, whole, keep, send, dx2, dcout, dgain, x2, h3, y, dh3,
):
    step = pl.program_id(0)
    width = x1.shape[1]

    @pl.when(step == 0)
    def _():
        x = x1[...] + nn(cout[...], wco[...])
        x2[...] = x
        h3[...] = (x * inv_rms(x) * gains[2:3]).astype(BF)
        y[...] = jnp.zeros_like(y)
        dh3[...] = jnp.zeros_like(dh3)

    u = nn(h3[...], win[...])
    t = jnp.tanh(GELU_C * (u + GELU_D * (u * u * u)))
    act = (0.5 * u * (1.0 + t)).astype(BF)
    y[...] += nn(act, wout[...])
    slope = 0.5 * (1.0 + t) + 0.5 * u * (1.0 - t * t) * (GELU_C * (1.0 + 3.0 * GELU_D * (u * u)))
    du = (nt(dy[...], wout[...]) * slope).astype(BF)
    dh3[...] += nt(du, win[...])

    @pl.when(step < WHOLE_STEPS)
    def _():
        whole[:, :width] = tn(h3[...], du).astype(BF)
        whole[:, width:] = tn(act, dy[...]).astype(BF)

    @pl.when(step >= WHOLE_STEPS)
    def _():
        part_ways(keep, send, slice(0, width), tn(h3[...], du), scal[2], chips)
        part_ways(keep, send, slice(width, None), tn(act, dy[...]), scal[2], chips)

    @pl.when(step == steps - 1)
    def _():
        x = x2[...]
        out[...] = (x + y[...]).astype(BF)
        dx, per_row = rms_back(x, gains[2:3], dh3[...])
        dx = dx + dy[...].astype(F32)
        dx2[...] = dx
        dgain[...] = column_sum(per_row, 2)
        dcout[...] = nt(dx.astype(BF), wco[...]).astype(BF)


def cross_backward(slots, ck, cv, cq, dcout, wck, wcv, dck, dcv, dcq, gn, qp, dop, dqp):
    rows, width = cq.shape
    groups = rows // SPAN + 1
    own_rows = ck.shape[0] - NEIGH * RET
    qp[...] = shift_in(cq[...].astype(F32), groups).astype(BF)
    dop[...] = shift_in(dcout[...].astype(F32), groups).astype(BF)
    for g in range(groups):
        places = [entry_rows(slots, g, n, own_rows) for n in range(NEIGH)]
        at = slice(g * SPAN, (g + 1) * SPAN)
        for quad in range(width // QUAD):
            cols = slice(quad * QUAD, (quad + 1) * QUAD)
            keys = window(ck, places, cols)
            q4 = by_heads(qp[at, cols])
            do4 = by_heads(dop[at, cols])
            s = nt(q4, keys)
            p = jnp.exp(s - jnp.max(s, axis=-1, keepdims=True))
            p = p * (1.0 / jnp.sum(p, axis=-1, keepdims=True))
            dp = nt(do4, window(cv, places, cols))
            ds = (p * (dp - jnp.sum(p * dp, axis=-1, keepdims=True))).astype(BF)
            dqp[at, cols] = from_heads(nn(ds, keys)) * SCALE
            dk = tn(ds, q4).astype(BF)
            dv = tn(p.astype(BF), do4).astype(BF)
            for n in range(NEIGH):
                part = slice(n * RET, (n + 1) * RET)
                dck[places[n], cols] = dk[part]
                dcv[places[n], cols] = dv[part]
    dcq[...] = shift_out(dqp[...], rows).astype(BF)
    gn[...] = (nt(dck[...], wck[...]) + nt(dcv[...], wcv[...])).astype(BF)


def branch_backward(
    chips, scal, att, x1, h2, dx2, dcq, nall, dck, dcv, dgain, cout, q, k, v, lse,
    wo, wcq, gains,
    keep, send, dx1, dgain_out, dq, dk, dv, bias, st, gt, datt,
):
    rows, width = x1.shape

    def put(u, total):
        part_ways(keep, send, slice(u * width, (u + 1) * width), total, scal[2], chips)

    dx, per_row = rms_back(x1[...], gains[1:2], nt(dcq[...], wcq[...]))
    dx = dx + dx2[...]
    dx1[...] = dx
    da = dx.astype(BF)
    dgain_out[...] = dgain[...] + column_sum(per_row, 1)
    datt[...] = nt(da, wo[...]).astype(BF)
    put(0, tn(att[...], da))
    put(1, tn(h2[...], dcq[...]))
    put(2, tn(nall[...], dck[...]))
    put(3, tn(nall[...], dcv[...]))
    put(4, tn(cout[...], dx2[...].astype(BF)))
    heads = QUAD // HEAD
    bias[...] = self_bias(scal[0], scal[1], rows, k.shape[0])
    lane = lax.broadcasted_iota(jnp.int32, (rows, LANES), 1)
    stats = lse[...]
    for quad in range(width // QUAD):
        cols = slice(quad * QUAD, (quad + 1) * QUAD)
        kq, vq = k[:, cols], v[:, cols]
        q4, da4 = by_heads(q[:, cols]), by_heads(datt[:, cols])
        for h in range(heads):
            at = slice(h * rows, (h + 1) * rows)
            level = jnp.sum(
                jnp.where(lane == quad * heads + h, stats, 0.0), axis=-1, keepdims=True
            )
            p = jnp.exp(nt(q4[at], kq) + bias[...] - level)
            dp = nt(da4[at], vq)
            ds = p * (dp - jnp.sum(p * dp, axis=-1, keepdims=True))
            st[at, :] = ds.astype(BF)
            gt[at, :] = p.astype(BF)
        dq[:, cols] = (from_heads(nn(st[...], kq)) * SCALE).astype(BF)
        dk[:, cols] = tn(st[...], q4).astype(BF)
        dv[:, cols] = tn(gt[...], da4).astype(BF)


def self_weights(chips, scal, h1, dq, dk, dv, dgain, wq, wk, wv, gain_cols, keep, send):
    rows, width = dq.shape
    products = jnp.zeros((width, 1), F32)
    for u, (rows_of, grad, w) in enumerate(((rows, dq, wq), (None, dk, wk), (None, dv, wv))):
        total = tn(h1[0:rows_of], grad[...])
        cols = slice(u * width, (u + 1) * width)
        part_ways(keep, send, cols, total, scal[2], chips)
        products = products + jnp.sum(total * w[...].astype(F32), axis=-1, keepdims=True)
    first = products / gain_cols[:, 0:1].astype(F32)
    lane = lax.broadcasted_iota(jnp.int32, (width, LANES), 1)
    total = jnp.where(lane == 0, first, dgain[...])
    total = jnp.concatenate([total, jnp.zeros_like(total)], axis=1)
    part_ways(keep, send, slice(3 * width, None), total, scal[2], chips)


def self_inputs(peers, dq, dk, dv, wq, wk, wv, keep, send):
    rows = dq.shape[0]
    for block in range(peers):
        at = slice(block * rows, (block + 1) * rows)
        part = nt(dk[at], wk[...]) + nt(dv[at], wv[...])
        if block == 0:
            part = part + nt(dq[...], wq[...])
        to = slice(block // 2 * rows, (block // 2 + 1) * rows)
        if block % 2 == 0:
            keep[to] = part
        else:
            send[to] = part.astype(BF)


def fold_kernel(places, count, scal, *refs):
    ins, outs = refs[: 2 * count], refs[2 * count :]
    start = 0
    for i in range(count):
        kept, came = ins[2 * i], ins[2 * i + 1]
        cols = slice(start, start + kept.shape[-1])
        start = start + kept.shape[-1]
        for k in range(places):
            at = pl.ds(lax.bitwise_xor(scal[0], k), 1)
            total = kept[:, at].astype(F32) + came[:, at].astype(F32)
            outs[k][:, :, cols] = total[:, 0].astype(BF)


def last_kernel(count, *refs):
    total = refs[0][...].astype(F32)
    for came in refs[1:count]:
        total = total + came[...].astype(F32)
    start = 0
    for out in refs[count:]:
        out[...] = total[:, start : start + out.shape[1]]
        start = start + out.shape[1]


def params():
    return pltpu.CompilerParams(vmem_limit_bytes=VMEM_LIMIT)


def scalar_spec():
    return pl.BlockSpec(memory_space=pltpu.SMEM)


def vmem_spec():
    return pl.BlockSpec(memory_space=pltpu.VMEM)


def unit_spec(width, u):
    return pl.BlockSpec((width, width), lambda i, u=u: (0, u))


def full_spec(shape):
    return pl.BlockSpec(shape, lambda i: (0,) * len(shape))


def sds(shape, dtype):
    return jax.ShapeDtypeStruct(shape, dtype)


def call(kernel, ins, outs, scratch, grid=(1,), us=10, after=()):
    specs = [full_spec(a.shape) if s is None else s for a, s in ins]
    specs = specs + [pl.BlockSpec(memory_space=pl.ANY)] * len(after)
    out_specs = [full_spec(o.shape) if s is None else s for o, s in outs]
    moved = sum(o.size * o.dtype.itemsize for o, _ in outs)

    def wrapped(*refs):
        kernel(*refs[: len(ins)], *refs[len(ins) + len(after) :])

    return pl.pallas_call(
        wrapped,
        grid=grid,
        in_specs=specs,
        out_specs=out_specs,
        out_shape=[o for o, _ in outs],
        scratch_shapes=scratch,
        compiler_params=params(),
        cost_estimate=pl.CostEstimate(
            flops=int(us * 1.1e9), bytes_accessed=2 * moved, transcendentals=0
        ),
    )(*[a for a, _ in ins], *after)


def split_four(x):
    rows, total = x.shape
    return x.reshape(rows, total // 4, 4).swapaxes(1, 2).reshape(rows, total)


def join_four(x):
    rows, total = x.shape
    return x.reshape(rows, 4, total // 4).swapaxes(1, 2).reshape(rows, total)


def exchange(x, by):
    peers = lax.axis_size("dp")
    return lax.ppermute(x, "dp", [(i, i ^ by) for i in range(peers)])


def shifted(x, by):
    peers = lax.axis_size("dp")
    return lax.ppermute(x, "dp", [(i, i + by) for i in range(peers) if 0 <= i + by < peers])


def axes_of():
    dp, nbr = lax.axis_size("dp"), lax.axis_size("nbr")
    y_count = 1 << ((nbr.bit_length() - 2) // 2)
    parts = {"x": dp // 2, "c": 2, "z": nbr // y_count, "y": y_count}
    strides = {"x": 2, "c": 1, "z": y_count, "y": 1}
    return parts, strides


def place_on(name):
    parts, strides = axes_of()
    return lax.rem(lax.axis_index("dp" if name in "xc" else "nbr") // strides[name], parts[name])


def pass_on(x, name, k=1):
    _, strides = axes_of()
    axis = "dp" if name in "xc" else "nbr"
    pairs = [(i, i ^ (k * strides[name])) for i in range(lax.axis_size(axis))]
    return lax.ppermute(x, axis, pairs)


def column_block(cols):
    return max(c for c in range(LANES, min(cols, 1024) + 1, LANES) if cols % c == 0)


def fold(pairs, left, name):
    parts, _ = axes_of()
    before, after = left.split(name)
    own = pairs[0][0].shape[0]
    for axis in left:
        own = own // parts[axis]
    lead, inner, places = 1, own, parts[name]
    for axis in before:
        lead = lead * parts[axis]
    for axis in after:
        inner = inner * parts[axis]
    arrays = [x.reshape(lead, places, inner, x.shape[1]) for pair in pairs for x in pair]
    cols = sum(pair[0].shape[1] for pair in pairs)
    block = column_block(cols) if len(pairs) == 1 else cols

    def spec(x):
        width = block if len(pairs) == 1 else x.shape[-1]
        return pl.BlockSpec(x.shape[:-1] + (width,), lambda i: (0,) * (x.ndim - 1) + (i,))

    out = sds((lead, inner, cols), BF)
    outs = call(
        functools.partial(fold_kernel, places, len(pairs)),
        [(place_on(name).reshape(1).astype(jnp.int32), scalar_spec())]
        + [(x, spec(x)) for x in arrays],
        [(out, pl.BlockSpec((lead, inner, block), lambda i: (0, 0, i)))] * places,
        [],
        grid=(cols // block,),
        us=3,
    )
    return [x.reshape(lead * inner, cols) for x in outs]


def fold_last(parts_of, widths):
    kept, sends = parts_of[0], parts_of[1:]
    came = [pass_on(x, "z", k + 1) for k, x in enumerate(sends)]
    return call(
        functools.partial(last_kernel, 1 + len(came)),
        [(x, None) for x in [kept] + came],
        [(sds((kept.shape[0], w), F32), None) for w in widths],
        [],
        us=2,
    )


def body(
    tokens,
    neighbours,
    lengths,
    slots,
    grad_out,
    w_query,
    w_key,
    w_value,
    w_attn_out,
    w_cross_query,
    w_cross_key,
    w_cross_value,
    w_cross_out,
    w_mlp_in,
    w_mlp_out,
    gain_attn,
    gain_cross,
    gain_mlp,
):
    peers = lax.axis_size("dp")
    _, rows, width = tokens.shape
    inner = w_mlp_in.shape[1]
    part = w_query.shape[0]
    key_count = rows * peers
    groups = rows // SPAN + 1
    halo = NEIGH * RET

    gains = jnp.stack([gain_attn, gain_cross, gain_mlp], axis=1)
    gains = jnp.pad(gains, ((0, 0), (0, LANES - 3)))
    shard = jnp.concatenate(
        [
            w_query,
            w_key,
            w_value,
            w_attn_out,
            w_cross_query,
            w_cross_key,
            w_cross_value,
            w_cross_out,
            split_four(w_mlp_in),
            w_mlp_out.reshape(part, inner),
            gains,
        ],
        axis=1,
    ).astype(BF)
    mats = lax.all_gather(shard, ("dp", "nbr"), axis=0, tiled=True)
    gain_rows = jnp.pad(mats[:, 8 * width + 2 * inner :][:, :3].astype(F32).T, ((0, 5), (0, 0)))

    def mat(u):
        return (mats, unit_spec(width, u))

    own_tokens = tokens[0]
    xall = jnp.concatenate([own_tokens] + [exchange(own_tokens, k) for k in range(1, peers)])
    entries = lax.all_to_all(neighbours, "nbr", split_axis=0, concat_axis=1, tiled=True)[0]
    own_rows = entries.shape[0]
    slot_list = slots.reshape(-1)
    last = [
        lax.dynamic_slice_in_dim(entries, slot_list[slot_list.shape[0] - NEIGH + n] * RET, RET)
        for n in range(NEIGH)
    ]
    behind = shifted(jnp.concatenate(last), 1)
    nall = jnp.concatenate([entries, behind])
    n_rows = own_rows + halo

    chips = peers // 2
    scal = jnp.stack(
        [lax.axis_index("dp").astype(jnp.int32), lengths[0], place_on("c").astype(jnp.int32)]
    )
    dy = grad_out[0]

    def low(*shape):
        return (sds(shape, BF), None)

    def wide(*shape):
        return (sds(shape, F32), None)

    h1, q, k, v, att, lse, x1, h2, cq = call(
        self_forward,
        [
            (scal, scalar_spec()), (xall, None), mat(U_Q), mat(U_K), mat(U_V), mat(U_O),
            mat(U_CQ), (gain_rows, None),
        ],
        [
            low(key_count, width), low(rows, width), low(key_count, width),
            low(key_count, width), low(rows, width), wide(rows, LANES), wide(rows, width),
            low(rows, width), low(rows, width),
        ],
        [pltpu.VMEM((rows, key_count), F32)],
        us=13,
    )
    ck, cv, cout = call(
        cross_forward,
        [(slot_list, scalar_spec()), (nall, None), mat(U_CK), mat(U_CV), (cq, None)],
        [low(n_rows, width), low(n_rows, width), low(rows, width)],
        [pltpu.VMEM((groups * SPAN, width), BF), pltpu.VMEM((groups * SPAN, width), F32)],
    )
    blocks = inner // width
    steps = blocks
    half = width // 2
    wide_block = 2 * width
    n_part = blocks - WHOLE_STEPS

    def ahead(first):
        return pl.BlockSpec((width, width), lambda i: (0, first + i))

    parted = (
        sds((half, n_part * wide_block), BF),
        pl.BlockSpec((half, wide_block), lambda i: (0, jnp.maximum(i - WHOLE_STEPS, 0))),
    )
    out, whole, mlp, mlp_send, dx2, dcout, dgain = call(
        functools.partial(mlp_both, steps, chips),
        [
            (scal, scalar_spec()), (x1, None), (cout, None), (dy, None), mat(U_CO),
            (mats, ahead(U_IN)), (mats, ahead(U_IN + blocks)), (gain_rows, None),
        ],
        [
            low(rows, width),
            (
                sds((width, WHOLE_STEPS * wide_block), BF),
                pl.BlockSpec((width, wide_block), lambda i: (0, jnp.minimum(i, WHOLE_STEPS - 1))),
            ),
            parted, parted,
            wide(rows, width), low(rows, width), wide(width, LANES),
        ],
        [
            pltpu.VMEM((rows, width), F32), pltpu.VMEM((rows, width), BF),
            pltpu.VMEM((rows, width), F32), pltpu.VMEM((rows, width), F32),
        ],
        grid=(steps,), us=16,
    )
    whole_sum = lax.psum_scatter(whole, ("dp", "nbr"), scatter_dimension=0, tiled=True)
    mlp = fold([(mlp, pass_on(mlp_send, "c"))], "xzy", "x")

    dck, dcv, dcq, gn = call(
        cross_backward,
        [
            (slot_list, scalar_spec()), (ck, None), (cv, None), (cq, None), (dcout, None),
            mat(U_CK), mat(U_CV),
        ],
        [low(n_rows, width), low(n_rows, width), low(rows, width), low(n_rows, width)],
        [
            pltpu.VMEM((groups * SPAN, width), BF), pltpu.VMEM((groups * SPAN, width), BF),
            pltpu.VMEM((groups * SPAN, width), F32),
        ],
        us=16,
    )
    ahead_part = shifted(gn[own_rows:], -1)
    placed = gn[:own_rows].reshape(-1, RET, width)
    entry = jnp.arange(placed.shape[0], dtype=jnp.int32)[:, None, None]
    for n in range(NEIGH):
        extra = ahead_part[n * RET : (n + 1) * RET].astype(F32)
        here = entry == slot_list[slot_list.shape[0] - NEIGH + n]
        placed = placed + jnp.where(here, extra[None], 0.0)
    placed = placed.astype(BF).reshape(neighbours.shape)
    pieces = []
    for i in range(2):
        piece = placed[:, :, i * (width // 2) : (i + 1) * (width // 2)]
        pieces.append(lax.all_to_all(piece, "nbr", split_axis=0, concat_axis=0, tiled=True))
    grad_nbr = jnp.concatenate(pieces, axis=2)

    came = pass_on(mlp[1], "x")
    branch, branch_send, dx1, dgain, dq, dk, dv = call(
        functools.partial(branch_backward, chips),
        [
            (scal, scalar_spec()), (att, None), (x1, None), (h2, None), (dx2, None),
            (dcq, None), (nall, None), (dck, None), (dcv, None), (dgain, None), (cout, None),
            (q, None), (k, None), (v, None), (lse, None), mat(U_O), mat(U_CQ),
            (gain_rows, None),
        ],
        [
            low(half, 5 * width), low(half, 5 * width), wide(rows, width), wide(width, LANES),
            low(rows, width), low(key_count, width), low(key_count, width),
        ],
        [
            pltpu.VMEM((rows, key_count), F32),
            pltpu.VMEM((QUAD // HEAD * rows, key_count), BF),
            pltpu.VMEM((QUAD // HEAD * rows, key_count), BF),
            pltpu.VMEM((rows, width), BF),
        ],
        us=26,
    )
    mlp = fold([(mlp[0], came)], "zy", "y")
    came = pass_on(mlp[1], "y")
    branch_came = pass_on(branch_send, "c")
    rest_cols = 3 * width + 2 * LANES
    rest, rest_send = call(
        functools.partial(self_weights, chips),
        [
            (scal, scalar_spec()), (h1, None), (dq, None), (dk, None), (dv, None),
            (dgain, None), mat(U_Q), mat(U_K), mat(U_V),
            (mats, pl.BlockSpec((width, LANES), lambda i: (0, (8 * width + 2 * inner) // LANES))),
        ],
        [low(half, rest_cols), low(half, rest_cols)],
        [],
        us=9,
    )
    branch = fold([(branch, branch_came)], "xzy", "x")
    dh, dh_send = call(
        functools.partial(self_inputs, peers),
        [(dq, None), (dk, None), (dv, None), mat(U_Q), mat(U_K), mat(U_V)],
        [wide(key_count // 2, width), low(key_count // 2, width)],
        [],
        us=6,
        after=[branch[1]],
    )
    rest = fold([(rest, pass_on(rest_send, "c"))], "xzy", "y")
    branch = fold([(branch[0], pass_on(branch[1], "x"))], "zy", "y")
    mlp = fold([(mlp[0], came)], "z", "z")
    part_sum = fold_last(mlp, [n_part * wide_block])[0]
    rest = fold([(rest[0], pass_on(rest[1], "y"))], "xz", "x")
    tail = fold(
        [(branch[0], pass_on(branch[1], "y")), (rest[0], pass_on(rest[1], "x"))], "z", "z"
    )
    g_o, g_cq, g_ck, g_cv, g_co, g_q, g_k, g_v, g_gains = fold_last(
        tail, [width] * 8 + [2 * LANES]
    )
    sums = jnp.concatenate([whole_sum.astype(F32), part_sum], axis=1)
    sums = sums.reshape(part, blocks, 2, width)

    dh = (dh + exchange(dh_send, 1).astype(F32)).reshape(-1, rows, width)
    by = 2
    while by < peers:
        dh = dh[0::2] + exchange(dh[1::2].astype(BF), by).astype(F32)
        by = 2 * by
    dh = dh[0]
    back, _ = rms_back(own_tokens.astype(F32), gain_rows[0:1], dh)
    grad_tokens = (dx1 + back).astype(BF)

    return (
        out[None],
        grad_tokens[None],
        grad_nbr,
        g_q,
        g_k,
        g_v,
        g_o,
        g_cq,
        g_ck,
        g_cv,
        g_co,
        join_four(sums[:, :, 0].reshape(part, inner)),
        sums[:, :, 1].reshape(blocks * part, width),
        g_gains[:, 0],
        g_gains[:, 1],
        g_gains[:, 2],
    )


def solution(mesh):
    rows = P(("dp", "nbr"), None)
    vector = P(("dp", "nbr"))
    seq = P("nbr", "dp", None)
    nbr = P(None, ("dp", "nbr"), None)
    return jax.shard_map(
        body,
        mesh=mesh,
        in_specs=(seq, nbr, P("nbr"), seq, seq) + (rows,) * 10 + (vector,) * 3,
        out_specs=(seq, seq, nbr) + (rows,) * 10 + (vector,) * 3,
        check_vma=False,
    )
```

```python
import functools

import jax
import jax.numpy as jnp
from jax import lax
from jax.experimental import pallas as pl
from jax.experimental.pallas import tpu as pltpu
from jax.sharding import PartitionSpec as P

HEAD = 64
SPAN = 64
NEIGH = 2
RET = 128
QUAD = 256
LANES = 128

EPSILON = 1e-06
SCALE = 0.125
MASKED = -1e30
GELU_C = 0.7978845608
GELU_D = 0.044715

BF = jnp.bfloat16
F32 = jnp.float32
VMEM_LIMIT = 60 * 1024 * 1024

WHOLE_STEPS = 3
U_Q, U_K, U_V, U_O, U_CQ, U_CK, U_CV, U_CO, U_IN = range(9)


def nn(a, b):
    return lax.dot_general(a, b, (((1,), (0,)), ((), ())), preferred_element_type=F32)


def nt(a, b):
    return lax.dot_general(a, b, (((1,), (1,)), ((), ())), preferred_element_type=F32)


def tn(a, b):
    return lax.dot_general(a, b, (((0,), (0,)), ((), ())), preferred_element_type=F32)


def inv_rms(x):
    return lax.rsqrt(jnp.mean(x * x, axis=-1, keepdims=True) + EPSILON)


def rms_back(x, gain, dz):
    r = inv_rms(x)
    n = x * r
    dzg = dz * gain
    dx = r * (dzg - n * jnp.mean(dzg * n, axis=-1, keepdims=True))
    return dx, dz * n


def column_sum(values, column):
    rows = values.shape[0]
    pick = (lax.broadcasted_iota(jnp.int32, (rows, LANES), 1) == column).astype(BF)
    high = values.astype(BF)
    low = (values - high.astype(F32)).astype(BF)
    return tn(high, pick) + tn(low, pick)


def head_lane(rows):
    return lax.broadcasted_iota(jnp.int32, (rows, QUAD), 1) // HEAD


def only_head(x, h):
    return jnp.where(head_lane(x.shape[0]) == h, x, jnp.zeros_like(x))


def by_heads(x):
    return jnp.concatenate([only_head(x, h) for h in range(QUAD // HEAD)], axis=0)


def from_heads(x):
    rows = x.shape[0] // (QUAD // HEAD)
    lane = head_lane(rows)
    out = x[:rows]
    for h in range(1, QUAD // HEAD):
        out = jnp.where(lane == h, x[h * rows : (h + 1) * rows], out)
    return out


def self_bias(place, length, rows, key_count):
    shape = (rows, key_count)
    key = lax.broadcasted_iota(jnp.int32, shape, 1)
    key_pos = lax.bitwise_xor(place, key // rows) * rows + lax.rem(key, rows)
    query_pos = place * rows + lax.broadcasted_iota(jnp.int32, shape, 0)
    return jnp.where((key_pos <= query_pos) & (key_pos < length), 0.0, MASKED).astype(F32)


def self_forward(
    scal, xall, wq, wk, wv, wo, wcq, gains, h1, q, k, v, att, lse, x1, h2, cq, bias
):
    rows = q.shape[0]
    key_count, width = xall.shape
    x = xall[...].astype(F32)
    h1[...] = (x * inv_rms(x) * gains[0:1]).astype(BF)
    q[...] = (nn(h1[0:rows], wq[...]) * SCALE).astype(BF)
    k[...] = nn(h1[...], wk[...]).astype(BF)
    v[...] = nn(h1[...], wv[...]).astype(BF)
    bias[...] = self_bias(scal[0], scal[1], rows, key_count)
    lane = lax.broadcasted_iota(jnp.int32, (rows, LANES), 1)
    stats = jnp.zeros((rows, LANES), F32)
    for quad in range(width // QUAD):
        cols = slice(quad * QUAD, (quad + 1) * QUAD)
        qq, kq, vq = q[:, cols], k[:, cols], v[:, cols]
        total = jnp.zeros((rows, QUAD), F32)
        for h in range(QUAD // HEAD):
            s = nt(only_head(qq, h), kq) + bias[...]
            m = jnp.max(s, axis=-1, keepdims=True)
            p = jnp.exp(s - m)
            z = jnp.sum(p, axis=-1, keepdims=True)
            o = nn(p.astype(BF), vq) * (1.0 / z)
            total = jnp.where(head_lane(rows) == h, o, total)
            stats = jnp.where(lane == quad * (QUAD // HEAD) + h, m + jnp.log(z), stats)
        att[:, cols] = total.astype(BF)
    lse[...] = stats
    mid = x[0:rows] + nn(att[...], wo[...])
    x1[...] = mid
    h2[...] = (mid * inv_rms(mid) * gains[1:2]).astype(BF)
    cq[...] = (nn(h2[...], wcq[...]) * SCALE).astype(BF)


def shift_in(x, groups):
    pad = jnp.zeros((groups * SPAN - x.shape[0], x.shape[1]), F32)
    return pltpu.roll(jnp.concatenate([x, pad], axis=0), 1, 0)


def shift_out(x, rows):
    return pltpu.roll(x, x.shape[0] - 1, 0)[0:rows]


def entry_rows(slots, group, n, own_rows):
    if group == 0:
        return pl.ds(own_rows + n * RET, RET)
    return pl.ds(pl.multiple_of(slots[(group - 1) * NEIGH + n] * RET, RET), RET)


def window(ref, places, cols):
    return jnp.concatenate([ref[at, cols] for at in places], axis=0)


def cross_forward(slots, nall, wck, wcv, cq, ck, cv, cout, qp, op):
    rows, width = cq.shape
    groups = rows // SPAN + 1
    own_rows = nall.shape[0] - NEIGH * RET
    ck[...] = nn(nall[...], wck[...]).astype(BF)
    cv[...] = nn(nall[...], wcv[...]).astype(BF)
    qp[...] = shift_in(cq[...].astype(F32), groups).astype(BF)
    for g in range(groups):
        places = [entry_rows(slots, g, n, own_rows) for n in range(NEIGH)]
        at = slice(g * SPAN, (g + 1) * SPAN)
        for quad in range(width // QUAD):
            cols = slice(quad * QUAD, (quad + 1) * QUAD)
            s = nt(by_heads(qp[at, cols]), window(ck, places, cols))
            p = jnp.exp(s - jnp.max(s, axis=-1, keepdims=True))
            p = p * (1.0 / jnp.sum(p, axis=-1, keepdims=True))
            op[at, cols] = from_heads(nn(p.astype(BF), window(cv, places, cols)))
    cout[...] = shift_out(op[...], rows).astype(BF)


def part_ways(keep, send, cols, total, core, chips):
    rows = total.shape[0] // (2 * chips)
    for x in range(chips):
        first = total[2 * x * rows : (2 * x + 1) * rows]
        second = total[(2 * x + 1) * rows : (2 * x + 2) * rows]
        at = slice(x * rows, (x + 1) * rows)
        keep[at, cols] = jnp.where(core == 0, first, second).astype(BF)
        send[at, cols] = jnp.where(core == 0, second, first).astype(BF)


def mlp_both(
    steps, chips, scal, x1, cout, dy, wco, win, wout, gains,
    out, whole, keep, send, dx2, dcout, dgain, x2, h3, y, dh3,
):
    step = pl.program_id(0)
    width = x1.shape[1]

    @pl.when(step == 0)
    def _():
        x = x1[...] + nn(cout[...], wco[...])
        x2[...] = x
        h3[...] = (x * inv_rms(x) * gains[2:3]).astype(BF)
        y[...] = jnp.zeros_like(y)
        dh3[...] = jnp.zeros_like(dh3)

    u = nn(h3[...], win[...])
    t = jnp.tanh(GELU_C * (u + GELU_D * (u * u * u)))
    act = (0.5 * u * (1.0 + t)).astype(BF)
    y[...] += nn(act, wout[...])
    slope = 0.5 * (1.0 + t) + 0.5 * u * (1.0 - t * t) * (GELU_C * (1.0 + 3.0 * GELU_D * (u * u)))
    du = (nt(dy[...], wout[...]) * slope).astype(BF)
    dh3[...] += nt(du, win[...])

    @pl.when(step < WHOLE_STEPS)
    def _():
        whole[:, :width] = tn(h3[...], du).astype(BF)
        whole[:, width:] = tn(act, dy[...]).astype(BF)

    @pl.when(step >= WHOLE_STEPS)
    def _():
        part_ways(keep, send, slice(0, width), tn(h3[...], du), scal[2], chips)
        part_ways(keep, send, slice(width, None), tn(act, dy[...]), scal[2], chips)

    @pl.when(step == steps - 1)
    def _():
        x = x2[...]
        out[...] = (x + y[...]).astype(BF)
        dx, per_row = rms_back(x, gains[2:3], dh3[...])
        dx = dx + dy[...].astype(F32)
        dx2[...] = dx
        dgain[...] = column_sum(per_row, 2)
        dcout[...] = nt(dx.astype(BF), wco[...]).astype(BF)


def cross_backward(slots, ck, cv, cq, dcout, wck, wcv, dck, dcv, dcq, gn, qp, dop, dqp):
    rows, width = cq.shape
    groups = rows // SPAN + 1
    own_rows = ck.shape[0] - NEIGH * RET
    qp[...] = shift_in(cq[...].astype(F32), groups).astype(BF)
    dop[...] = shift_in(dcout[...].astype(F32), groups).astype(BF)
    for g in range(groups):
        places = [entry_rows(slots, g, n, own_rows) for n in range(NEIGH)]
        at = slice(g * SPAN, (g + 1) * SPAN)
        for quad in range(width // QUAD):
            cols = slice(quad * QUAD, (quad + 1) * QUAD)
            keys = window(ck, places, cols)
            q4 = by_heads(qp[at, cols])
            do4 = by_heads(dop[at, cols])
            s = nt(q4, keys)
            p = jnp.exp(s - jnp.max(s, axis=-1, keepdims=True))
            p = p * (1.0 / jnp.sum(p, axis=-1, keepdims=True))
            dp = nt(do4, window(cv, places, cols))
            ds = (p * (dp - jnp.sum(p * dp, axis=-1, keepdims=True))).astype(BF)
            dqp[at, cols] = from_heads(nn(ds, keys)) * SCALE
            dk = tn(ds, q4).astype(BF)
            dv = tn(p.astype(BF), do4).astype(BF)
            for n in range(NEIGH):
                part = slice(n * RET, (n + 1) * RET)
                dck[places[n], cols] = dk[part]
                dcv[places[n], cols] = dv[part]
    dcq[...] = shift_out(dqp[...], rows).astype(BF)
    gn[...] = (nt(dck[...], wck[...]) + nt(dcv[...], wcv[...])).astype(BF)


def branch_backward(
    chips, scal, att, x1, h2, dx2, dcq, nall, dck, dcv, dgain, cout, q, k, v, lse,
    wo, wcq, gains,
    keep, send, dx1, dgain_out, dq, dk, dv, bias, st, gt, datt,
):
    rows, width = x1.shape

    def put(u, total):
        part_ways(keep, send, slice(u * width, (u + 1) * width), total, scal[2], chips)

    dx, per_row = rms_back(x1[...], gains[1:2], nt(dcq[...], wcq[...]))
    dx = dx + dx2[...]
    dx1[...] = dx
    da = dx.astype(BF)
    dgain_out[...] = dgain[...] + column_sum(per_row, 1)
    datt[...] = nt(da, wo[...]).astype(BF)
    put(0, tn(att[...], da))
    put(1, tn(h2[...], dcq[...]))
    put(2, tn(nall[...], dck[...]))
    put(3, tn(nall[...], dcv[...]))
    put(4, tn(cout[...], dx2[...].astype(BF)))
    heads = QUAD // HEAD
    bias[...] = self_bias(scal[0], scal[1], rows, k.shape[0])
    lane = lax.broadcasted_iota(jnp.int32, (rows, LANES), 1)
    stats = lse[...]
    for quad in range(width // QUAD):
        cols = slice(quad * QUAD, (quad + 1) * QUAD)
        kq, vq = k[:, cols], v[:, cols]
        q4, da4 = by_heads(q[:, cols]), by_heads(datt[:, cols])
        each = datt[:, cols].astype(F32) * att[:, cols].astype(F32)
        for h in range(heads):
            at = slice(h * rows, (h + 1) * rows)
            level = jnp.sum(
                jnp.where(lane == quad * heads + h, stats, 0.0), axis=-1, keepdims=True
            )
            delta = jnp.sum(only_head(each, h), axis=-1, keepdims=True)
            p = jnp.exp(nt(q4[at], kq) + bias[...] - level)
            gt[at, :] = p.astype(BF)
            st[at, :] = (p * (nt(da4[at], vq) - delta)).astype(BF)
        dq[:, cols] = (from_heads(nn(st[...], kq)) * SCALE).astype(BF)
        dk[:, cols] = tn(st[...], q4).astype(BF)
        dv[:, cols] = tn(gt[...], da4).astype(BF)


def self_weights(chips, scal, h1, dq, dk, dv, dgain, wq, wk, wv, gain_cols, keep, send):
    rows, width = dq.shape
    products = jnp.zeros((width, 1), F32)
    for u, (rows_of, grad, w) in enumerate(((rows, dq, wq), (None, dk, wk), (None, dv, wv))):
        total = tn(h1[0:rows_of], grad[...])
        cols = slice(u * width, (u + 1) * width)
        part_ways(keep, send, cols, total, scal[2], chips)
        products = products + jnp.sum(total * w[...].astype(F32), axis=-1, keepdims=True)
    first = products / gain_cols[:, 0:1].astype(F32)
    lane = lax.broadcasted_iota(jnp.int32, (width, LANES), 1)
    total = jnp.where(lane == 0, first, dgain[...])
    total = jnp.concatenate([total, jnp.zeros_like(total)], axis=1)
    part_ways(keep, send, slice(3 * width, None), total, scal[2], chips)


def self_inputs(peers, dq, dk, dv, wq, wk, wv, keep, send):
    rows = dq.shape[0]
    for block in range(peers):
        at = slice(block * rows, (block + 1) * rows)
        part = nt(dk[at], wk[...]) + nt(dv[at], wv[...])
        if block == 0:
            part = part + nt(dq[...], wq[...])
        to = slice(block // 2 * rows, (block // 2 + 1) * rows)
        if block % 2 == 0:
            keep[to] = part
        else:
            send[to] = part.astype(BF)


def fold_kernel(places, count, scal, *refs):
    ins, outs = refs[: 2 * count], refs[2 * count :]
    start = 0
    for i in range(count):
        kept, came = ins[2 * i], ins[2 * i + 1]
        cols = slice(start, start + kept.shape[-1])
        start = start + kept.shape[-1]
        for k in range(places):
            at = pl.ds(lax.bitwise_xor(scal[0], k), 1)
            outs[k][:, :, cols] = (kept[:, at] + came[:, at])[:, 0]


def last_kernel(count, *refs):
    total = refs[0][...].astype(F32)
    for came in refs[1:count]:
        total = total + came[...].astype(F32)
    start = 0
    for out in refs[count:]:
        out[...] = total[:, start : start + out.shape[1]]
        start = start + out.shape[1]


def params():
    return pltpu.CompilerParams(vmem_limit_bytes=VMEM_LIMIT)


def scalar_spec():
    return pl.BlockSpec(memory_space=pltpu.SMEM)


def vmem_spec():
    return pl.BlockSpec(memory_space=pltpu.VMEM)


def unit_spec(width, u):
    return pl.BlockSpec((width, width), lambda i, u=u: (0, u))


def full_spec(shape):
    return pl.BlockSpec(shape, lambda i: (0,) * len(shape))


def sds(shape, dtype):
    return jax.ShapeDtypeStruct(shape, dtype)


def call(kernel, ins, outs, scratch, grid=(1,), us=10, after=()):
    specs = [full_spec(a.shape) if s is None else s for a, s in ins]
    specs = specs + [pl.BlockSpec(memory_space=pl.ANY)] * len(after)
    out_specs = [full_spec(o.shape) if s is None else s for o, s in outs]
    moved = sum(o.size * o.dtype.itemsize for o, _ in outs)

    def wrapped(*refs):
        kernel(*refs[: len(ins)], *refs[len(ins) + len(after) :])

    return pl.pallas_call(
        wrapped,
        grid=grid,
        in_specs=specs,
        out_specs=out_specs,
        out_shape=[o for o, _ in outs],
        scratch_shapes=scratch,
        compiler_params=params(),
        cost_estimate=pl.CostEstimate(
            flops=int(us * 1.1e9), bytes_accessed=2 * moved, transcendentals=0
        ),
    )(*[a for a, _ in ins], *after)


def split_four(x):
    rows, total = x.shape
    return x.reshape(rows, total // 4, 4).swapaxes(1, 2).reshape(rows, total)


def join_four(x):
    rows, total = x.shape
    return x.reshape(rows, 4, total // 4).swapaxes(1, 2).reshape(rows, total)


def exchange(x, by):
    peers = lax.axis_size("dp")
    return lax.ppermute(x, "dp", [(i, i ^ by) for i in range(peers)])


def shifted(x, by):
    peers = lax.axis_size("dp")
    return lax.ppermute(x, "dp", [(i, i + by) for i in range(peers) if 0 <= i + by < peers])


def axes_of():
    dp, nbr = lax.axis_size("dp"), lax.axis_size("nbr")
    y_count = 1 << ((nbr.bit_length() - 2) // 2)
    parts = {"x": dp // 2, "c": 2, "z": nbr // y_count, "y": y_count}
    strides = {"x": 2, "c": 1, "z": y_count, "y": 1}
    return parts, strides


def place_on(name):
    parts, strides = axes_of()
    return lax.rem(lax.axis_index("dp" if name in "xc" else "nbr") // strides[name], parts[name])


def pass_on(x, name, k=1):
    _, strides = axes_of()
    axis = "dp" if name in "xc" else "nbr"
    pairs = [(i, i ^ (k * strides[name])) for i in range(lax.axis_size(axis))]
    return lax.ppermute(x, axis, pairs)


def column_block(cols):
    return max(c for c in range(LANES, min(cols, 1024) + 1, LANES) if cols % c == 0)


def fold(pairs, left, name):
    parts, _ = axes_of()
    before, after = left.split(name)
    own = pairs[0][0].shape[0]
    for axis in left:
        own = own // parts[axis]
    lead, inner, places = 1, own, parts[name]
    for axis in before:
        lead = lead * parts[axis]
    for axis in after:
        inner = inner * parts[axis]
    arrays = [x.reshape(lead, places, inner, x.shape[1]) for pair in pairs for x in pair]
    cols = sum(pair[0].shape[1] for pair in pairs)
    block = column_block(cols) if len(pairs) == 1 else cols

    def spec(x):
        width = block if len(pairs) == 1 else x.shape[-1]
        return pl.BlockSpec(x.shape[:-1] + (width,), lambda i: (0,) * (x.ndim - 1) + (i,))

    out = sds((lead, inner, cols), BF)
    outs = call(
        functools.partial(fold_kernel, places, len(pairs)),
        [(place_on(name).reshape(1).astype(jnp.int32), scalar_spec())]
        + [(x, spec(x)) for x in arrays],
        [(out, pl.BlockSpec((lead, inner, block), lambda i: (0, 0, i)))] * places,
        [],
        grid=(cols // block,),
        us=3,
    )
    return [x.reshape(lead * inner, cols) for x in outs]


def fold_last(parts_of, widths):
    kept, sends = parts_of[0], parts_of[1:]
    came = [pass_on(x, "z", k + 1) for k, x in enumerate(sends)]
    return call(
        functools.partial(last_kernel, 1 + len(came)),
        [(x, None) for x in [kept] + came],
        [(sds((kept.shape[0], w), F32), None) for w in widths],
        [],
        us=2,
    )


def body(
    tokens,
    neighbours,
    lengths,
    slots,
    grad_out,
    w_query,
    w_key,
    w_value,
    w_attn_out,
    w_cross_query,
    w_cross_key,
    w_cross_value,
    w_cross_out,
    w_mlp_in,
    w_mlp_out,
    gain_attn,
    gain_cross,
    gain_mlp,
):
    peers = lax.axis_size("dp")
    _, rows, width = tokens.shape
    inner = w_mlp_in.shape[1]
    part = w_query.shape[0]
    key_count = rows * peers
    groups = rows // SPAN + 1
    halo = NEIGH * RET

    gains = jnp.stack([gain_attn, gain_cross, gain_mlp], axis=1)
    gains = jnp.pad(gains, ((0, 0), (0, LANES - 3)))
    shard = jnp.concatenate(
        [
            w_query,
            w_key,
            w_value,
            w_attn_out,
            w_cross_query,
            w_cross_key,
            w_cross_value,
            w_cross_out,
            split_four(w_mlp_in),
            w_mlp_out.reshape(part, inner),
            gains,
        ],
        axis=1,
    ).astype(BF)
    mats = lax.all_gather(shard, ("dp", "nbr"), axis=0, tiled=True)
    gain_rows = jnp.pad(mats[:, 8 * width + 2 * inner :][:, :3].astype(F32).T, ((0, 5), (0, 0)))

    def mat(u):
        return (mats, unit_spec(width, u))

    own_tokens = tokens[0]
    xall = jnp.concatenate([own_tokens] + [exchange(own_tokens, k) for k in range(1, peers)])
    entries = lax.all_to_all(neighbours, "nbr", split_axis=0, concat_axis=1, tiled=True)[0]
    own_rows = entries.shape[0]
    slot_list = slots.reshape(-1)
    last = [
        lax.dynamic_slice_in_dim(entries, slot_list[slot_list.shape[0] - NEIGH + n] * RET, RET)
        for n in range(NEIGH)
    ]
    behind = shifted(jnp.concatenate(last), 1)
    nall = jnp.concatenate([entries, behind])
    n_rows = own_rows + halo

    chips = peers // 2
    scal = jnp.stack(
        [lax.axis_index("dp").astype(jnp.int32), lengths[0], place_on("c").astype(jnp.int32)]
    )
    dy = grad_out[0]

    def low(*shape):
        return (sds(shape, BF), None)

    def wide(*shape):
        return (sds(shape, F32), None)

    h1, q, k, v, att, lse, x1, h2, cq = call(
        self_forward,
        [
            (scal, scalar_spec()), (xall, None), mat(U_Q), mat(U_K), mat(U_V), mat(U_O),
            mat(U_CQ), (gain_rows, None),
        ],
        [
            low(key_count, width), low(rows, width), low(key_count, width),
            low(key_count, width), low(rows, width), wide(rows, LANES), wide(rows, width),
            low(rows, width), low(rows, width),
        ],
        [pltpu.VMEM((rows, key_count), F32)],
        us=13,
    )
    ck, cv, cout = call(
        cross_forward,
        [(slot_list, scalar_spec()), (nall, None), mat(U_CK), mat(U_CV), (cq, None)],
        [low(n_rows, width), low(n_rows, width), low(rows, width)],
        [pltpu.VMEM((groups * SPAN, width), BF), pltpu.VMEM((groups * SPAN, width), F32)],
    )
    blocks = inner // width
    steps = blocks
    half = width // 2
    wide_block = 2 * width
    n_part = blocks - WHOLE_STEPS

    def ahead(first):
        return pl.BlockSpec((width, width), lambda i: (0, first + i))

    parted = (
        sds((half, n_part * wide_block), BF),
        pl.BlockSpec((half, wide_block), lambda i: (0, jnp.maximum(i - WHOLE_STEPS, 0))),
    )
    out, whole, mlp, mlp_send, dx2, dcout, dgain = call(
        functools.partial(mlp_both, steps, chips),
        [
            (scal, scalar_spec()), (x1, None), (cout, None), (dy, None), mat(U_CO),
            (mats, ahead(U_IN)), (mats, ahead(U_IN + blocks)), (gain_rows, None),
        ],
        [
            low(rows, width),
            (
                sds((width, WHOLE_STEPS * wide_block), BF),
                pl.BlockSpec((width, wide_block), lambda i: (0, jnp.minimum(i, WHOLE_STEPS - 1))),
            ),
            parted, parted,
            wide(rows, width), low(rows, width), wide(width, LANES),
        ],
        [
            pltpu.VMEM((rows, width), F32), pltpu.VMEM((rows, width), BF),
            pltpu.VMEM((rows, width), F32), pltpu.VMEM((rows, width), F32),
        ],
        grid=(steps,), us=16,
    )
    whole_sum = lax.psum_scatter(whole, ("dp", "nbr"), scatter_dimension=0, tiled=True)
    mlp = fold([(mlp, pass_on(mlp_send, "c"))], "xzy", "x")

    dck, dcv, dcq, gn = call(
        cross_backward,
        [
            (slot_list, scalar_spec()), (ck, None), (cv, None), (cq, None), (dcout, None),
            mat(U_CK), mat(U_CV),
        ],
        [low(n_rows, width), low(n_rows, width), low(rows, width), low(n_rows, width)],
        [
            pltpu.VMEM((groups * SPAN, width), BF), pltpu.VMEM((groups * SPAN, width), BF),
            pltpu.VMEM((groups * SPAN, width), F32),
        ],
        us=16,
    )
    ahead_part = shifted(gn[own_rows:], -1)
    placed = gn[:own_rows].reshape(-1, RET, width)
    entry = jnp.arange(placed.shape[0], dtype=jnp.int32)[:, None, None]
    for n in range(NEIGH):
        extra = ahead_part[n * RET : (n + 1) * RET].astype(F32)
        here = entry == slot_list[slot_list.shape[0] - NEIGH + n]
        placed = placed + jnp.where(here, extra[None], 0.0)
    placed = placed.astype(BF).reshape(neighbours.shape)
    pieces = []
    for i in range(2):
        piece = placed[:, :, i * (width // 2) : (i + 1) * (width // 2)]
        pieces.append(lax.all_to_all(piece, "nbr", split_axis=0, concat_axis=0, tiled=True))
    grad_nbr = jnp.concatenate(pieces, axis=2)

    came = pass_on(mlp[1], "x")
    branch, branch_send, dx1, dgain, dq, dk, dv = call(
        functools.partial(branch_backward, chips),
        [
            (scal, scalar_spec()), (att, None), (x1, None), (h2, None), (dx2, None),
            (dcq, None), (nall, None), (dck, None), (dcv, None), (dgain, None), (cout, None),
            (q, None), (k, None), (v, None), (lse, None), mat(U_O), mat(U_CQ),
            (gain_rows, None),
        ],
        [
            low(half, 5 * width), low(half, 5 * width), wide(rows, width), wide(width, LANES),
            low(rows, width), low(key_count, width), low(key_count, width),
        ],
        [
            pltpu.VMEM((rows, key_count), F32),
            pltpu.VMEM((QUAD // HEAD * rows, key_count), BF),
            pltpu.VMEM((QUAD // HEAD * rows, key_count), BF),
            pltpu.VMEM((rows, width), BF),
        ],
        us=26,
    )
    mlp = fold([(mlp[0], came)], "zy", "y")
    came = pass_on(mlp[1], "y")
    branch_came = pass_on(branch_send, "c")
    rest_cols = 3 * width + 2 * LANES
    rest, rest_send = call(
        functools.partial(self_weights, chips),
        [
            (scal, scalar_spec()), (h1, None), (dq, None), (dk, None), (dv, None),
            (dgain, None), mat(U_Q), mat(U_K), mat(U_V),
            (mats, pl.BlockSpec((width, LANES), lambda i: (0, (8 * width + 2 * inner) // LANES))),
        ],
        [low(half, rest_cols), low(half, rest_cols)],
        [],
        us=9,
    )
    branch = fold([(branch, branch_came)], "xzy", "x")
    dh, dh_send = call(
        functools.partial(self_inputs, peers),
        [(dq, None), (dk, None), (dv, None), mat(U_Q), mat(U_K), mat(U_V)],
        [wide(key_count // 2, width), low(key_count // 2, width)],
        [],
        us=6,
        after=[branch[1]],
    )
    rest = fold([(rest, pass_on(rest_send, "c"))], "xzy", "y")
    branch = fold([(branch[0], pass_on(branch[1], "x"))], "zy", "y")
    mlp = fold([(mlp[0], came)], "z", "z")
    part_sum = fold_last(mlp, [n_part * wide_block])[0]
    rest = fold([(rest[0], pass_on(rest[1], "y"))], "xz", "x")
    tail = fold(
        [(branch[0], pass_on(branch[1], "y")), (rest[0], pass_on(rest[1], "x"))], "z", "z"
    )
    g_o, g_cq, g_ck, g_cv, g_co, g_q, g_k, g_v, g_gains = fold_last(
        tail, [width] * 8 + [2 * LANES]
    )
    sums = jnp.concatenate([whole_sum.astype(F32), part_sum], axis=1)
    sums = sums.reshape(part, blocks, 2, width)

    dh = (dh + exchange(dh_send, 1).astype(F32)).reshape(-1, rows, width)
    by = 2
    while by < peers:
        dh = dh[0::2] + exchange(dh[1::2].astype(BF), by).astype(F32)
        by = 2 * by
    dh = dh[0]
    back, _ = rms_back(own_tokens.astype(F32), gain_rows[0:1], dh)
    grad_tokens = (dx1 + back).astype(BF)

    return (
        out[None],
        grad_tokens[None],
        grad_nbr,
        g_q,
        g_k,
        g_v,
        g_o,
        g_cq,
        g_ck,
        g_cv,
        g_co,
        join_four(sums[:, :, 0].reshape(part, inner)),
        sums[:, :, 1].reshape(blocks * part, width),
        g_gains[:, 0],
        g_gains[:, 1],
        g_gains[:, 2],
    )


def solution(mesh):
    rows = P(("dp", "nbr"), None)
    vector = P(("dp", "nbr"))
    seq = P("nbr", "dp", None)
    nbr = P(None, ("dp", "nbr"), None)
    return jax.shard_map(
        body,
        mesh=mesh,
        in_specs=(seq, nbr, P("nbr"), seq, seq) + (rows,) * 10 + (vector,) * 3,
        out_specs=(seq, seq, nbr) + (rows,) * 10 + (vector,) * 3,
        check_vma=False,
    )
```
